256 devices in a mesh: blk: 16 (over x, z_hi, core), uly: 16 (over y, z_lo).
Axes of the slice: x: 4, y: 4, z: 8 (z_hi: 2, z_lo: 4; z = z_hi * 4 + z_lo), core: 2. Of those that a mesh axis runs over, the one named last changes fastest.
Arguments:
- queries: bfloat16 [16384, 4096], P(('blk', 'uly')), may hold values from -8 to 8
- gate: bfloat16 [16384, 4096], P(('blk', 'uly')), may hold values from -6 to 6
- keys: bfloat16 [16384, 512], P(('blk', 'uly')), may hold values from -8 to 8
- values: bfloat16 [16384, 512], P(('blk', 'uly')), may hold values from -6 to 6
- q_gain: float32 [256], replicated, may hold values from 0.7 to 5
- k_gain: float32 [256], replicated, may hold values from 0.7 to 5
- span_of: int32 [32], replicated, may hold values from 0 to 31, each once
Outputs:
- gated: bfloat16 [16384, 4096], P(('blk', 'uly'))
The draws below stay inside these ranges and needn't reach their ends.
Inputs may be any that keep to these rules, and one draw needn't show every extreme that they name: span_of is a permutation of 0 to 31.
All inputs are finite; a program needn't handle non-finite values.
Results may differ from the reference program's by a relative error of at most 0.0085.
The reference program's roundings to bfloat16 on the way (of `q_rot`, `k_rot`, `weights` and `attended`) count: a program that leaves them out, or rounds other values in their place, can miss the bound.
Values may be sent and summed in bfloat16 or wider, within the bound.
No kernel may reach another device: no remote copies, remote signals or barrier semaphores. Data moves between devices by JAX's collectives and lax.ppermute only.
A program may use at most 64 MiB of HBM per device.

```python
import jax
import jax.numpy as jnp
from jax import lax

HEAD_DIM = 256
KV_HEADS = 2
ROTARY = 64
HEADS = 16
TOKENS = 16384
SPAN_ROWS = 512
SPAN_COUNT = 32


def draw_keys(key, part):
    key = jax.random.fold_in(key, 3)
    fresh = jax.random.normal(key, (TOKENS, KV_HEADS * HEAD_DIM), jnp.float32)
    return jnp.clip(fresh, -6.0, 6.0).astype(jnp.bfloat16)


def draw_queries(key, part):
    key = jax.random.fold_in(key, 5)
    fresh = jax.random.normal(key, (TOKENS, HEADS * HEAD_DIM), jnp.float32)
    return jnp.clip(fresh, -6.0, 6.0).astype(jnp.bfloat16)


def draw_q_gain(key, part):
    key = jax.random.fold_in(key, 7)
    return jax.random.uniform(key, (HEAD_DIM,), jnp.float32, 0.7, 1.4)


def draw_k_gain(key, part):
    key = jax.random.fold_in(key, 9)
    return jax.random.uniform(key, (HEAD_DIM,), jnp.float32, 0.7, 1.4)


def block_scale(stream_key, extent, cuts, smallest, top_value):
    def one(axis_at, parts):
        heights = jax.random.uniform(jax.random.fold_in(jax.random.fold_in(stream_key, 6), axis_at), (parts,), jnp.float32, smallest / len(cuts), top_value / len(cuts))
        return jnp.repeat(jnp.exp(heights), extent[axis_at] // parts).reshape((-1,) + (1,) * (len(extent) - axis_at - 1))

    factor_of = one(*cuts[0])
    for cut in cuts[1:]:
        factor_of = factor_of * one(*cut)
    return factor_of


def bell_draw(rng, extent, scale, bound, shards=(), kind=jnp.bfloat16):
    loudness = block_scale(rng, extent, shards, -0.22, 0.18) if shards else 1.0
    drawn = jax.random.normal(rng, extent, jnp.float32) * scale * loudness
    return jnp.minimum(jnp.maximum(drawn, -bound), bound).astype(kind)


def setup_inputs(seed: int = 0) -> dict:
    key_list = jax.random.split(jax.random.key(seed), 8)
    queries = draw_queries(jax.random.fold_in(key_list[7], 71), 0)
    gate = bell_draw(key_list[1], (TOKENS, HEADS * HEAD_DIM), 1.5, 6.0, ((0, 256),))
    keys = draw_keys(jax.random.fold_in(key_list[7], 71), 0)
    values = bell_draw(key_list[3], (TOKENS, KV_HEADS * HEAD_DIM), 1.0, 6.0, ((0, 256),))
    q_gain = draw_q_gain(jax.random.fold_in(key_list[7], 71), 0)
    k_gain = draw_k_gain(jax.random.fold_in(key_list[7], 71), 0)
    span_of = jax.random.permutation(key_list[6], SPAN_COUNT).astype(jnp.int32)
    return {"queries": queries, "gate": gate, "keys": keys, "values": values, "q_gain": q_gain, "k_gain": k_gain, "span_of": span_of}


ROPE_BASE = 10000000.0
MASKED = -1e+30

def normed_rotated(source, gain, positions):
    row_count = source.shape[0]
    feature_count = gain.shape[0]
    pieces = source.astype(jnp.float32).reshape(row_count, -1, feature_count)
    pieces = pieces * lax.rsqrt(lax.optimization_barrier(jnp.mean(pieces * pieces, axis=-1, keepdims=True)) + 1e-06) * gain
    halfway = ROTARY // 2
    frequency = ROPE_BASE ** (-2.0 * jnp.arange(halfway, dtype=jnp.float32) / ROTARY)
    angles = positions.astype(jnp.float32)[:, None] * frequency[None, :]
    cosine = jnp.cos(angles)[:, None, :]
    sine = jnp.sin(angles)[:, None, :]
    leading = pieces[..., :halfway]
    trailing = pieces[..., halfway:ROTARY]
    turned = jnp.concatenate([leading * cosine - trailing * sine, trailing * cosine + leading * sine, pieces[..., ROTARY:]], axis=-1)
    return turned.reshape(row_count, -1).astype(jnp.bfloat16)

def reference(queries, gate, keys, values, q_gain, k_gain, span_of):
    row_index = jnp.arange(TOKENS, dtype=jnp.int32)
    positions = span_of[row_index // SPAN_ROWS] * SPAN_ROWS + row_index % SPAN_ROWS
    q_rot = normed_rotated(queries, q_gain, positions)
    k_rot = normed_rotated(keys, k_gain, positions)
    group_size = HEADS // KV_HEADS
    factor = HEAD_DIM ** (-0.5)
    within = jnp.arange(SPAN_ROWS, dtype=jnp.int32)

    def one_span(slot):
        q_block = lax.dynamic_slice_in_dim(q_rot, (slot * SPAN_ROWS).astype(jnp.int32), SPAN_ROWS, 0)
        q_block = q_block.astype(jnp.float32).reshape(SPAN_ROWS, KV_HEADS, group_size, HEAD_DIM)
        q_positions = span_of[slot] * SPAN_ROWS + within

        def visit(other, state):

            def update(current):
                running_max, running_sum, numerator = current
                offset = (other * SPAN_ROWS).astype(jnp.int32)
                k_block = lax.dynamic_slice_in_dim(k_rot, offset, SPAN_ROWS, 0).astype(jnp.float32).reshape(SPAN_ROWS, KV_HEADS, HEAD_DIM)
                v_block = lax.dynamic_slice_in_dim(values, offset, SPAN_ROWS, 0).astype(jnp.float32).reshape(SPAN_ROWS, KV_HEADS, HEAD_DIM)
                k_positions = span_of[other] * SPAN_ROWS + within
                scores = jnp.einsum('qkgd,pkd->kgqp', q_block, k_block) * factor
                allowed = k_positions[None, :] <= q_positions[:, None]
                scores = jnp.where(allowed, scores, MASKED)
                new_max = jnp.maximum(running_max, lax.optimization_barrier(jnp.max(scores, axis=-1)))
                weights = jnp.where(allowed, jnp.exp(scores - new_max[..., None]), 0.0)
                fading = jnp.exp(running_max - new_max)
                new_sum = running_sum * fading + lax.optimization_barrier(jnp.sum(weights, axis=-1))
                rounded = lax.optimization_barrier(weights.astype(jnp.bfloat16)).astype(jnp.float32)
                new_numerator = numerator * fading[..., None] + jnp.einsum('kgqp,pkd->kgqd', rounded, v_block)
                return (new_max, new_sum, new_numerator)
            return lax.cond(span_of[other] <= span_of[slot], update, lambda kept: kept, state)
        initial = (jnp.full((KV_HEADS, group_size, SPAN_ROWS), MASKED, jnp.float32), jnp.zeros((KV_HEADS, group_size, SPAN_ROWS), jnp.float32), jnp.zeros((KV_HEADS, group_size, SPAN_ROWS, HEAD_DIM), jnp.float32))
        running_max, running_sum, numerator = lax.fori_loop(0, SPAN_COUNT, visit, initial)
        result = numerator / running_sum[..., None]
        return result.transpose(2, 0, 1, 3).reshape(SPAN_ROWS, HEADS * HEAD_DIM).astype(jnp.bfloat16)
    attended = lax.map(one_span, jnp.arange(SPAN_COUNT, dtype=jnp.int32)).reshape(TOKENS, HEADS * HEAD_DIM)
    attended = lax.optimization_barrier(attended)
    return (attended.astype(jnp.float32) * jax.nn.sigmoid(gate.astype(jnp.float32))).astype(jnp.bfloat16)
```

```python
import functools

import jax
import jax.numpy as jnp
from jax import lax
from jax.experimental import pallas as pl
from jax.experimental.pallas import tpu as pltpu
from jax.sharding import PartitionSpec as P

ROTARY = 64
ROPE_BASE = 10000000.0
EPSILON = 1e-06
LOG2E = 1.4426950408889634

GRID = (4, 2, 2, 4, 4)
AXES = ("blk", "uly")
ROWS = 64
DIM = 256
GROUP = 8
TILE = GROUP * ROWS
STATS = 16
SPAN = 512
CHUNK = 128
SHIFTS = (0, 1, 3, 2)

HIDDEN = -1e30
EMPTY = -1e25


def place_of(index):
    place = []
    for extent in reversed(GRID):
        place.append(index % extent)
        index //= extent
    return tuple(reversed(place))


def index_of(place):
    index = 0
    for extent, at in zip(GRID, place):
        index = index * extent + at
    return index


def send(array, target):
    count = index_of(tuple(extent - 1 for extent in GRID)) + 1
    route = [(i, index_of(target(*place_of(i)))) for i in range(count)]
    return lax.ppermute(array, AXES, route)


def to_line(flip):
    return lambda x, zh, c, y, zl: (x, zh, c, y, zl ^ flip)


def to_far(flip):
    return lambda x, zh, c, y, zl: (x, zh ^ 1, c, y, zl ^ flip)


def to_core(x, zh, c, y, zl):
    return (x, zh, c ^ 1, y, zl)


def to_ring(shift, phase):
    def target(x, zh, c, y, zl):
        if c == phase:
            return ((x + shift) % 4, zh, c, y, zl)
        return (x, zh, c, (y + shift) % 4, zl)

    return target


def whole(*shape):
    return pl.BlockSpec(shape, lambda *_: (0,) * len(shape))


def turned(piece, gain, cosine, sine):
    piece = piece.astype(jnp.float32)
    scale = lax.rsqrt(jnp.mean(piece * piece, axis=-1, keepdims=True) + EPSILON)
    piece = piece * scale * gain
    front = piece[:, :128]
    lane = lax.broadcasted_iota(jnp.int32, front.shape, 1)
    half = ROTARY // 2
    partner = jnp.where(lane < half, pltpu.roll(front, 128 - half, 1), pltpu.roll(front, half, 1))
    front = front * cosine + partner * sine
    return jnp.concatenate([front, piece[:, 128:]], axis=-1).astype(jnp.bfloat16)


def keys_kernel(meta, keys, values, gain, cosine, sine, own, other):
    side = meta[40]
    for which, out in ((0, own), (1, other)):
        head = side if which == 0 else 1 - side
        columns = pl.ds(pl.multiple_of(head * DIM, DIM), DIM)
        out[:ROWS] = turned(keys[:, columns], gain[...], cosine[...], sine[...])
        out[ROWS:] = values[:, columns]


def queries_kernel(meta, queries, gain, cosine, sine, own, other):
    side = meta[40]
    for which, out in ((0, own), (1, other)):
        head = side if which == 0 else 1 - side
        for member in range(GROUP):
            columns = pl.ds(pl.multiple_of((head * GROUP + member) * DIM, DIM), DIM)
            piece = turned(queries[:, columns], gain[...], cosine[...], sine[...])
            out[member * ROWS : (member + 1) * ROWS] = piece * jnp.bfloat16(DIM**-0.5)


def attend_kernel(first, last, buffers, key_base, query_base, meta, queries, *refs):
    refs = list(refs)
    stores = [refs.pop(0) for _ in range(buffers)]
    if not first:
        top_in, total_in, sum_in = refs.pop(0), refs.pop(0), refs.pop(0)
    if last:
        out, top, total, acc, order = refs
    else:
        top, total, acc, order = refs
    per_store = stores[0].shape[0]
    chunks = buffers * per_store
    tile = pl.program_id(0)
    start = meta[query_base + tile]
    side = meta[40]

    if first:
        top[...] = jnp.full(top.shape, EMPTY, jnp.float32)
        total[...] = jnp.zeros(total.shape, jnp.float32)
        acc[...] = jnp.zeros(acc.shape, jnp.float32)
    else:
        top[...] = top_in[...]
        total[...] = total_in[...]
        acc[...] = sum_in[...]

    def sort(j, carry):
        full_count, partial = carry
        key_start = meta[key_base + j]
        full = key_start + (CHUNK - 1) <= start
        some = jnp.logical_and(key_start <= start + (ROWS - 1), jnp.logical_not(full))
        order[full_count] = j
        return (full_count + full.astype(jnp.int32), jnp.where(some, j, partial))

    full_count, partial = lax.fori_loop(0, chunks, sort, (jnp.int32(0), jnp.int32(-1)))

    def fetch(j, part):
        rows = slice(part * CHUNK, (part + 1) * CHUNK)
        if buffers == 1:
            return stores[0][j, rows]
        picked = stores[0][lax.rem(j, per_store), rows]
        for n in range(1, buffers):
            picked = jnp.where(j // per_store == n, stores[n][lax.rem(j, per_store), rows], picked)
        return picked

    def step(picks, limits):
        keys = jnp.concatenate([fetch(j, 0) for j in picks], axis=0)
        values = jnp.concatenate([fetch(j, 1) for j in picks], axis=0)
        for sub in range(TILE // 128):
            rows = slice(sub * 128, (sub + 1) * 128)
            scores = (
                lax.dot_general(
                    queries[0, rows],
                    keys,
                    (((1,), (1,)), ((), ())),
                    preferred_element_type=jnp.float32,
                )
                * LOG2E
            )
            parts = [scores[:, n * 128 : (n + 1) * 128] for n in range(len(picks))]
            if limits is not None:
                row = lax.broadcasted_iota(jnp.int32, (128, 128), 0)
                lane = lax.broadcasted_iota(jnp.int32, (128, 128), 1)
                gap = (lane ^ (side * ROWS)) - (row & (ROWS - 1))
                parts = [
                    jnp.where(gap <= limit, part, HIDDEN) for part, limit in zip(parts, limits)
                ]
            before = top[0, rows]
            peak = functools.reduce(jnp.maximum, parts)
            now = jnp.maximum(before, jnp.max(peak, axis=-1, keepdims=True))
            fading = jnp.exp2(before - now)
            weights = [jnp.exp2(part - now) for part in parts]
            total[0, rows] = total[0, rows] * fading + functools.reduce(jnp.add, weights)
            top[0, rows] = now
            product = jnp.dot(
                jnp.concatenate(weights, axis=-1).astype(jnp.bfloat16),
                values,
                preferred_element_type=jnp.float32,
            )
            acc[0, rows] = acc[0, rows] * jnp.concatenate([fading, fading], axis=-1) + product

    def both(n, carry):
        step([order[2 * n], order[2 * n + 1]], None)
        return carry

    lax.fori_loop(0, full_count // 2, both, 0)
    odd = lax.rem(full_count, 2) == 1
    has_partial = partial >= 0

    @pl.when(jnp.logical_or(odd, has_partial))
    def _():
        left = jnp.where(odd, order[jnp.maximum(full_count - 1, 0)], 0)
        right = jnp.maximum(partial, 0)
        left_limit = jnp.where(odd, jnp.int32(1 << 20), jnp.int32(-(1 << 20)))
        right_limit = jnp.where(
            has_partial, start - meta[key_base + right], jnp.int32(-(1 << 20))
        )
        step([left, right], [left_limit, right_limit])

    if last:
        logs = []
        for sub in range(TILE // 128):
            rows = slice(sub * 128, (sub + 1) * 128)
            sums = jnp.maximum(jnp.sum(total[0, rows], axis=-1, keepdims=True), 1e-37)
            out[0, rows] = (acc[0, rows] / sums).astype(jnp.bfloat16)
            level = top[0, rows] + jnp.log2(sums)
            logs.append(level.T[:1])
        out[0, TILE:] = packed(logs)


def packed(logs):
    level = jnp.concatenate(logs, axis=0)
    high = level.astype(jnp.bfloat16).astype(jnp.float32)
    middle = (level - high).astype(jnp.bfloat16).astype(jnp.float32)
    low = level - high - middle
    rows = jnp.concatenate([high, middle, low, jnp.zeros_like(low)], axis=0)
    return jnp.concatenate([rows, jnp.zeros_like(rows)], axis=-1).astype(jnp.bfloat16)


def unpacked(rows):
    rows = rows[:, :128].astype(jnp.float32)
    return rows[0:4] + rows[4:8] + rows[8:12]


def blend(left, right):
    a, b = unpacked(left), unpacked(right)
    peak = jnp.maximum(a, b)
    a, b = jnp.exp2(a - peak), jnp.exp2(b - peak)
    both = a + b
    return a / both, b / both, peak + jnp.log2(both)


def column(shares, n):
    share = jnp.broadcast_to(shares[n : n + 1], (128, 128)).T
    return jnp.concatenate([share, share], axis=-1)


def join_kernel(mine, theirs, *outs):
    for r, out in enumerate(outs):
        a, b, level = blend(mine[r, TILE:], theirs[r, TILE:])
        for n in range(TILE // 128):
            rows = slice(n * 128, (n + 1) * 128)
            left = mine[r, rows].astype(jnp.float32) * column(a, n)
            right = theirs[r, rows].astype(jnp.float32) * column(b, n)
            out[rows] = (left + right).astype(jnp.bfloat16)
        out[TILE:] = packed([level])


def finish_kernel(meta, near0, near1, far0, far1, gate, out):
    side = meta[40]
    for which, (left_ref, right_ref) in enumerate(((near0, far0), (near1, far1))):
        head = side if which == 0 else 1 - side
        a, b, _ = blend(left_ref[TILE:], right_ref[TILE:])
        for n in range(TILE // 128):
            rows = slice(n * 128, (n + 1) * 128)
            left = left_ref[rows].astype(jnp.float32) * column(a, n)
            right = right_ref[rows].astype(jnp.float32) * column(b, n)
            attended = (left + right).astype(jnp.bfloat16).astype(jnp.float32)
            for m in range(2):
                at = (head * GROUP + 2 * n + m) * DIM
                columns = pl.ds(pl.multiple_of(at, DIM), DIM)
                logits = gate[:, columns].astype(jnp.float32)
                gated = attended[m * ROWS : (m + 1) * ROWS] * jax.nn.sigmoid(logits)
                out[:, columns] = gated.astype(jnp.bfloat16)


SMEM = pl.BlockSpec(memory_space=pltpu.SMEM)
VMEM = pl.BlockSpec(memory_space=pltpu.VMEM)
BIG = pltpu.CompilerParams(vmem_limit_bytes=48 * 1024 * 1024)


def attend(meta, queries, stores, state, last, key_base, query_base):
    first = state is None
    buffers = len(stores)
    chunks = buffers * stores[0].shape[0]
    wide = lambda width: pl.BlockSpec((1, TILE, width), lambda i: (i, 0, 0))
    state_specs = [wide(128), wide(128), wide(DIM)]
    state_shapes = [jax.ShapeDtypeStruct((4, TILE, w), jnp.float32) for w in (128, 128, DIM)]
    scratch = [pltpu.SMEM((chunks + 8,), jnp.int32)]
    if last:
        out_specs = pl.BlockSpec((1, TILE + STATS, DIM), lambda i: (i, 0, 0))
        out_shape = jax.ShapeDtypeStruct((4, TILE + STATS, DIM), jnp.bfloat16)
        scratch = [pltpu.VMEM((1, TILE, w), jnp.float32) for w in (128, 128, DIM)] + scratch
    else:
        out_specs, out_shape = state_specs, state_shapes
    whole_store = pl.BlockSpec(stores[0].shape, lambda i: (0, 0, 0))
    return pl.pallas_call(
        functools.partial(attend_kernel, first, last, buffers, key_base, query_base),
        grid=(4,),
        in_specs=[SMEM, wide(DIM)] + [whole_store] * buffers + ([] if first else state_specs),
        out_specs=out_specs,
        out_shape=out_shape,
        scratch_shapes=scratch,
        compiler_params=BIG,
        cost_estimate=pl.CostEstimate(
            flops=4 * TILE * chunks * CHUNK * DIM * 4,
            bytes_accessed=4 << 20,
            transcendentals=4 * TILE * chunks * CHUNK,
        ),
    )(meta, queries, *stores, *(() if first else state))


def local(queries, gate, keys, values, q_gain, k_gain, span_of):
    index = lax.axis_index("blk") * 16 + lax.axis_index("uly")
    x, zh, c, y, zl = place_of(index)
    side, part = zl & 1, zl >> 1

    def first_position(xs, zhs, cs, ys, within):
        slot = ((xs * 2 + zhs) * 2 + cs) * 2 + (ys >> 1)
        return span_of[slot] * SPAN + (ys & 1) * 256 + within

    r = jnp.arange(8, dtype=jnp.int32)
    query_starts = first_position(x, zh, c ^ (r >> 2), y, (zl ^ (r & 3)) * ROWS)
    j = jnp.arange(32, dtype=jnp.int32)
    shifts = jnp.array(SHIFTS, jnp.int32)
    outer, inner = shifts[j >> 3], shifts[(j >> 1) & 3]
    xs = (x - jnp.where(c == 0, inner, outer)) % 4
    ys = (y - jnp.where(c == 0, outer, inner)) % 4
    key_starts = first_position(xs, zh ^ (j & 1), c, ys, part * CHUNK)
    meta = jnp.concatenate([query_starts, key_starts, jnp.full((8,), side, jnp.int32)])

    positions = query_starts[0] + jnp.arange(ROWS, dtype=jnp.int32)
    lane = jnp.arange(128, dtype=jnp.int32)
    frequency = ROPE_BASE ** (-2.0 * (lane % 32).astype(jnp.float32) / ROTARY)
    angles = positions.astype(jnp.float32)[:, None] * frequency[None, :]
    rotated = lane[None, :] < ROTARY
    cosine = jnp.where(rotated, jnp.cos(angles), 1.0)
    sine = jnp.sin(angles)
    sine = jnp.where(rotated, jnp.where(lane[None, :] < ROTARY // 2, -sine, sine), 0.0)

    pair = jax.ShapeDtypeStruct((2 * ROWS, DIM), jnp.bfloat16)
    kv_own, kv_other = pl.pallas_call(
        keys_kernel,
        in_specs=[SMEM] + [VMEM] * 5,
        out_specs=[VMEM] * 2,
        out_shape=[pair, pair],
        compiler_params=BIG,
    )(meta, keys, values, k_gain.reshape(1, DIM), cosine, sine)

    near = send(kv_other, to_line(1))
    far = send(kv_own, to_far(0))
    cross = send(kv_other, to_far(1))

    tile = jax.ShapeDtypeStruct((TILE, DIM), jnp.bfloat16)
    q_own, q_other = pl.pallas_call(
        queries_kernel,
        in_specs=[SMEM] + [VMEM] * 4,
        out_specs=[VMEM] * 2,
        out_shape=[tile, tile],
        compiler_params=BIG,
    )(meta, queries, q_gain.reshape(1, DIM), cosine, sine)

    base = jnp.concatenate(
        [
            kv_own[:ROWS],
            near[:ROWS],
            kv_own[ROWS:],
            near[ROWS:],
            far[:ROWS],
            cross[:ROWS],
            far[ROWS:],
            cross[ROWS:],
        ],
        axis=0,
    ).reshape(2, 2 * CHUNK, DIM)

    store = [base] + [send(base, to_ring(s, 0)) for s in SHIFTS[1:]]
    store = jnp.concatenate(store, axis=0)

    q_own, q_other, _ = lax.optimization_barrier((q_own, q_other, base))
    q_mine = jnp.stack(
        [q_own, send(q_other, to_line(1)), send(q_own, to_line(2)), send(q_other, to_line(3))]
    )
    arrived = [send(store, to_ring(s, 1)) for s in SHIFTS[1:]]
    q_theirs = send(q_mine, to_core)

    state_mine = attend(meta, q_mine, [store], None, False, 8, 0)
    state_theirs = attend(meta, q_theirs, [store], None, False, 8, 4)
    state_theirs = attend(meta, q_theirs, arrived[:2], state_theirs, False, 16, 4)
    state_mine = attend(meta, q_mine, arrived[:2], state_mine, False, 16, 0)
    out_theirs = attend(meta, q_theirs, arrived[2:], state_theirs, True, 32, 4)
    received = send(out_theirs, to_core)
    out_mine = attend(meta, q_mine, arrived[2:], state_mine, True, 32, 0)

    joint = jax.ShapeDtypeStruct((TILE + STATS, DIM), jnp.bfloat16)
    parts = pl.pallas_call(
        join_kernel,
        in_specs=[VMEM] * 2,
        out_specs=[VMEM] * 4,
        out_shape=[joint] * 4,
        compiler_params=BIG,
    )(out_mine, received)
    home = [parts[0]] + [send(parts[n], to_line(n)) for n in range(1, 4)]

    return pl.pallas_call(
        finish_kernel,
        in_specs=[SMEM] + [VMEM] * 5,
        out_specs=VMEM,
        out_shape=jax.ShapeDtypeStruct(queries.shape, jnp.bfloat16),
        compiler_params=BIG,
    )(meta, *home, gate)


def solution(mesh):
    rows = P(("blk", "uly"), None)
    in_specs = (rows, rows, rows, rows, P(), P(), P())
    return jax.shard_map(local, mesh=mesh, in_specs=in_specs, out_specs=rows, check_vma=False)
```

```python
import functools

import jax
import jax.numpy as jnp
from jax import lax
from jax.experimental import pallas as pl
from jax.experimental.pallas import tpu as pltpu
from jax.sharding import PartitionSpec as P

ROTARY = 64
ROPE_BASE = 10000000.0
EPSILON = 1e-06
LOG2E = 1.4426950408889634

GRID = (4, 2, 2, 4, 4)
AXES = ("blk", "uly")
ROWS = 64
DIM = 256
GROUP = 8
TILE = GROUP * ROWS
STATS = 16
SPAN = 512
CHUNK = 128
SHIFTS = (0, 1, 3, 2)

HIDDEN = -1e30
EMPTY = -1e25


def place_of(index):
    place = []
    for extent in reversed(GRID):
        place.append(index % extent)
        index //= extent
    return tuple(reversed(place))


def index_of(place):
    index = 0
    for extent, at in zip(GRID, place):
        index = index * extent + at
    return index


def send(array, target):
    count = index_of(tuple(extent - 1 for extent in GRID)) + 1
    route = [(i, index_of(target(*place_of(i)))) for i in range(count)]
    return lax.ppermute(array, AXES, route)


def to_mate(x, zh, c, y, zl):
    return (x, zh, c, y, zl ^ 1)


def to_far(x, zh, c, y, zl):
    return (x, zh ^ 1, c, y, zl)


def along_z(even):
    def target(x, zh, c, y, zl):
        z = (zh * 4 + zl + (-even if zl & 1 else even)) % 8
        return (x, z // 4, c, y, z % 4)

    return target


def to_core(x, zh, c, y, zl):
    return (x, zh, c ^ 1, y, zl)


def to_ring(shift, phase):
    def target(x, zh, c, y, zl):
        if c == phase:
            return ((x + shift) % 4, zh, c, y, zl)
        return (x, zh, c, (y + shift) % 4, zl)

    return target


def whole(*shape):
    return pl.BlockSpec(shape, lambda *_: (0,) * len(shape))


def turned(piece, gain, cosine, sine):
    piece = piece.astype(jnp.float32)
    scale = lax.rsqrt(jnp.mean(piece * piece, axis=-1, keepdims=True) + EPSILON)
    piece = piece * scale * gain
    front = piece[:, :128]
    lane = lax.broadcasted_iota(jnp.int32, front.shape, 1)
    half = ROTARY // 2
    partner = jnp.where(lane < half, pltpu.roll(front, 128 - half, 1), pltpu.roll(front, half, 1))
    front = front * cosine + partner * sine
    return jnp.concatenate([front, piece[:, 128:]], axis=-1).astype(jnp.bfloat16)


def keys_kernel(near, far, gain, cosine, sine, out):
    for t, pair in enumerate((near, far)):
        for n in range(2):
            rows = slice(n * ROWS, (n + 1) * ROWS)
            at = slice(t * CHUNK + n * ROWS, t * CHUNK + (n + 1) * ROWS)
            piece = pair[n * CHUNK : (n + 1) * CHUNK]
            out[t, rows] = turned(piece[:ROWS], gain[...], cosine[at], sine[at])
            out[t, CHUNK + n * ROWS : CHUNK + (n + 1) * ROWS] = piece[ROWS:]


def queries_kernel(own, mate, next_mate, following, gain, cosine, sine, out):
    for n, piece in enumerate((own, mate, next_mate, following)):
        at = slice(n * ROWS, (n + 1) * ROWS)
        for member in range(GROUP):
            columns = slice(member * DIM, (member + 1) * DIM)
            rows = slice((n % 2) * TILE + member * ROWS, (n % 2) * TILE + (member + 1) * ROWS)
            rotated = turned(piece[:, columns], gain[...], cosine[at], sine[at])
            out[n // 2, rows] = rotated * jnp.bfloat16(DIM**-0.5)


def attend_kernel(first, last, key_bases, query_base, meta, queries, *refs):
    refs = list(refs)
    stores = [refs.pop(0) for _ in key_bases]
    given = None if first else [refs.pop(0) for _ in range(3)]
    if last:
        out = refs.pop(0)
    top, total, acc, order = refs
    side = meta[40]

    def one_tile(tile, carry):
        start = meta[query_base + tile]
        if first:
            top[tile] = jnp.full(top.shape[1:], EMPTY, jnp.float32)
            total[tile] = jnp.zeros(total.shape[1:], jnp.float32)
            acc[tile] = jnp.zeros(acc.shape[1:], jnp.float32)
        else:
            for now, before in zip((top, total, acc), given):
                now[tile] = before[tile]

        def step(store, picks, limits):
            keys = jnp.concatenate([store[j, :CHUNK] for j in picks], axis=0)
            values = jnp.concatenate([store[j, CHUNK:] for j in picks], axis=0)
            for piece in range(2):
                rows = slice(piece * TILE, (piece + 1) * TILE)
                scores = lax.dot_general(
                    queries[tile, rows],
                    keys,
                    (((1,), (1,)), ((), ())),
                    preferred_element_type=jnp.float32,
                )
                scores = scores * LOG2E
                parts = [scores[:, n * CHUNK : (n + 1) * CHUNK] for n in range(len(picks))]
                if limits is not None:
                    row = lax.broadcasted_iota(jnp.int32, (TILE, CHUNK), 0)
                    lane = lax.broadcasted_iota(jnp.int32, (TILE, CHUNK), 1)
                    gap = (lane ^ (side * ROWS)) - (row & (ROWS - 1)) - (side ^ piece) * ROWS
                    parts = [
                        jnp.where(gap <= limit, part, HIDDEN) for part, limit in zip(parts, limits)
                    ]
                before = top[tile, rows]
                peak = functools.reduce(jnp.maximum, parts)
                now = jnp.maximum(before, jnp.max(peak, axis=-1, keepdims=True))
                fading = jnp.exp2(before - now)
                weights = [jnp.exp2(part - now) for part in parts]
                total[tile, rows] = total[tile, rows] * fading + functools.reduce(jnp.add, weights)
                top[tile, rows] = now
                product = jnp.dot(
                    jnp.concatenate(weights, axis=-1).astype(jnp.bfloat16),
                    values,
                    preferred_element_type=jnp.float32,
                )
                fading = jnp.concatenate([fading, fading], axis=-1)
                acc[tile, rows] = acc[tile, rows] * fading + product

        for store, key_base in zip(stores, key_bases):
            chunks = store.shape[0]

            def sort(j, carry):
                count, partial = carry
                key_start = meta[key_base + j]
                full = key_start + (CHUNK - 1) <= start
                some = jnp.logical_and(
                    key_start <= start + (2 * ROWS - 1), jnp.logical_not(full)
                )
                order[count] = j
                return (count + full.astype(jnp.int32), jnp.where(some, j, partial))

            count, partial = lax.fori_loop(0, chunks, sort, (jnp.int32(0), jnp.int32(-1)))

            @pl.when(count == chunks)
            def _():
                step(store, list(range(chunks)), None)

            @pl.when(jnp.logical_and(count >= 4, count < chunks))
            def _():
                step(store, [order[n] for n in range(4)], None)

            rest = jnp.where(count == chunks, 0, lax.rem(count, 4))
            base = count - rest
            has_partial = partial >= 0

            @pl.when(jnp.logical_or(rest > 0, has_partial))
            def _():
                picks, limits = [], []
                for n in range(4):
                    whole_one = n < rest
                    cut = jnp.logical_and(n == rest, has_partial)
                    pick = jnp.where(whole_one, order[base + n], jnp.where(cut, partial, 0))
                    reach = start - meta[key_base + pick]
                    picks.append(pick)
                    limits.append(
                        jnp.where(whole_one, 1 << 20, jnp.where(cut, reach, -(1 << 20)))
                    )
                step(store, picks, limits)

        if last:
            for piece in range(2):
                logs = []
                for sub in range(TILE // 128):
                    rows = slice(piece * TILE + sub * 128, piece * TILE + (sub + 1) * 128)
                    sums = jnp.sum(total[tile, rows], axis=-1, keepdims=True)
                    sums = jnp.maximum(sums, 1e-37)
                    result = (acc[tile, rows] / sums).astype(jnp.bfloat16)
                    out[2 * tile + piece, sub * 128 : (sub + 1) * 128] = result
                    level = top[tile, rows] + jnp.log2(sums)
                    logs.append(level.T[:1])
                out[2 * tile + piece, TILE:] = packed(logs)
        return carry

    lax.fori_loop(0, 2, one_tile, 0)


def packed(logs):
    level = jnp.concatenate(logs, axis=0)
    high = level.astype(jnp.bfloat16).astype(jnp.float32)
    middle = (level - high).astype(jnp.bfloat16).astype(jnp.float32)
    low = level - high - middle
    rows = jnp.concatenate([high, middle, low, jnp.zeros_like(low)], axis=0)
    return jnp.concatenate([rows, jnp.zeros_like(rows)], axis=-1).astype(jnp.bfloat16)


def unpacked(rows):
    rows = rows[:, :128].astype(jnp.float32)
    return rows[0:4] + rows[4:8] + rows[8:12]


def blend(left, right):
    a, b = unpacked(left), unpacked(right)
    peak = jnp.maximum(a, b)
    a, b = jnp.exp2(a - peak), jnp.exp2(b - peak)
    both = a + b
    return a / both, b / both, peak + jnp.log2(both)


def column(shares, n):
    share = jnp.broadcast_to(shares[n : n + 1], (128, 128)).T
    return jnp.concatenate([share, share], axis=-1)


def join_kernel(mine, theirs, *outs):
    for r, out in enumerate(outs):
        a, b, level = blend(mine[r, TILE:], theirs[r, TILE:])
        for n in range(TILE // 128):
            rows = slice(n * 128, (n + 1) * 128)
            left = mine[r, rows].astype(jnp.float32) * column(a, n)
            right = theirs[r, rows].astype(jnp.float32) * column(b, n)
            out[rows] = (left + right).astype(jnp.bfloat16)
        out[TILE:] = packed([level])


def finish_kernel(meta, near0, near1, far0, far1, gate, out):
    side = meta[40]
    for which, (left_ref, right_ref) in enumerate(((near0, far0), (near1, far1))):
        head = side if which == 0 else 1 - side
        a, b, _ = blend(left_ref[TILE:], right_ref[TILE:])
        for n in range(TILE // 128):
            rows = slice(n * 128, (n + 1) * 128)
            left = left_ref[rows].astype(jnp.float32) * column(a, n)
            right = right_ref[rows].astype(jnp.float32) * column(b, n)
            attended = (left + right).astype(jnp.bfloat16).astype(jnp.float32)
            for m in range(2):
                at = (head * GROUP + 2 * n + m) * DIM
                columns = pl.ds(pl.multiple_of(at, DIM), DIM)
                logits = gate[:, columns].astype(jnp.float32)
                gated = attended[m * ROWS : (m + 1) * ROWS] * jax.nn.sigmoid(logits)
                out[:, columns] = gated.astype(jnp.bfloat16)


SMEM = pl.BlockSpec(memory_space=pltpu.SMEM)
VMEM = pl.BlockSpec(memory_space=pltpu.VMEM)
BIG = pltpu.CompilerParams(vmem_limit_bytes=28 * 1024 * 1024)


def attend(meta, queries, stores, state, last, key_bases, query_base):
    first = state is None
    shapes = [(2, 2 * TILE, width) for width in (128, 128, DIM)]
    scratch = [pltpu.SMEM((16,), jnp.int32)]
    if last:
        out_shape = jax.ShapeDtypeStruct((4, TILE + STATS, DIM), jnp.bfloat16)
        out_specs = VMEM
        scratch = [pltpu.VMEM(shape, jnp.float32) for shape in shapes] + scratch
    else:
        out_shape = [jax.ShapeDtypeStruct(shape, jnp.float32) for shape in shapes]
        out_specs = [VMEM] * 3
    chunks = 8 * len(stores)
    return pl.pallas_call(
        functools.partial(attend_kernel, first, last, key_bases, query_base),
        in_specs=[SMEM] + [VMEM] * (1 + len(stores) + (0 if first else 3)),
        out_specs=out_specs,
        out_shape=out_shape,
        scratch_shapes=scratch,
        compiler_params=BIG,
        cost_estimate=pl.CostEstimate(
            flops=4 * 4 * TILE * chunks * CHUNK * DIM,
            bytes_accessed=4 << 20,
            transcendentals=4 * TILE * chunks * CHUNK,
        ),
    )(meta, queries, *stores, *(() if first else state))


def local(queries, gate, keys, values, q_gain, k_gain, span_of):
    index = lax.axis_index("blk") * 16 + lax.axis_index("uly")
    x, zh, c, y, zl = place_of(index)
    side, part = zl & 1, zl >> 1

    both = jnp.concatenate([keys, values], axis=0)
    left, right = both[:, :DIM], both[:, DIM:]
    kv_own = jnp.where(side == 0, left, right)
    kv_other = jnp.where(side == 0, right, left)
    near = jnp.concatenate([kv_own, send(kv_other, to_mate)], axis=0)
    far = send(near, to_far)

    left, right = queries[:, : GROUP * DIM], queries[:, GROUP * DIM :]
    q_own = jnp.where(side == 0, left, right)
    q_other = jnp.where(side == 0, right, left)
    q_raw = [send(q_other, to_mate), send(q_own, along_z(2)), send(q_other, along_z(-1))]
    far, q_raw = lax.optimization_barrier((far, q_raw))

    def first_position(xs, zhs, cs, ys, within):
        slot = ((xs * 2 + zhs) * 2 + cs) * 2 + (ys >> 1)
        return span_of[slot] * SPAN + (ys & 1) * 256 + within

    z_next = (zh * 4 + zl + jnp.where(side == 0, 7, 1)) % 8
    r = jnp.arange(8, dtype=jnp.int32)
    z_tile = jnp.where((r & 1) == 0, zh * 4 + zl, z_next)
    tile_starts = first_position(
        x, z_tile >> 2, c ^ ((r >> 1) & 1), y, ((z_tile & 3) >> 1) * CHUNK
    )
    j = jnp.arange(32, dtype=jnp.int32)
    shifts = jnp.array(SHIFTS, jnp.int32)
    outer, inner = shifts[j >> 3], shifts[(j >> 1) & 3]
    xs = (x - jnp.where(c == 0, inner, outer)) % 4
    ys = (y - jnp.where(c == 0, outer, inner)) % 4
    key_starts = first_position(xs, zh ^ (j & 1), c, ys, part * CHUNK)
    meta = jnp.concatenate([tile_starts, key_starts, jnp.full((8,), side, jnp.int32)])

    def rotation(positions):
        lane = jnp.arange(128, dtype=jnp.int32)
        frequency = ROPE_BASE ** (-2.0 * (lane % 32).astype(jnp.float32) / ROTARY)
        angles = positions.astype(jnp.float32)[:, None] * frequency[None, :]
        rotated = lane[None, :] < ROTARY
        cosine = jnp.where(rotated, jnp.cos(angles), 1.0)
        sine = jnp.sin(angles)
        sine = jnp.where(rotated, jnp.where(lane[None, :] < ROTARY // 2, -sine, sine), 0.0)
        return cosine, sine

    starts = jnp.concatenate([tile_starts[:2], key_starts[:2]])
    row = jnp.arange(2 * ROWS, dtype=jnp.int32) ^ (side * ROWS)
    cosine, sine = rotation((starts[:, None] + row[None, :]).reshape(-1))

    base = pl.pallas_call(
        keys_kernel,
        in_specs=[VMEM] * 5,
        out_specs=VMEM,
        out_shape=jax.ShapeDtypeStruct((2, 2 * CHUNK, DIM), jnp.bfloat16),
        compiler_params=BIG,
    )(near, far, k_gain.reshape(1, DIM), cosine[4 * ROWS :], sine[4 * ROWS :])

    q_mine = pl.pallas_call(
        queries_kernel,
        in_specs=[VMEM] * 7,
        out_specs=VMEM,
        out_shape=jax.ShapeDtypeStruct((2, 2 * TILE, DIM), jnp.bfloat16),
        compiler_params=BIG,
    )(q_own, *q_raw, q_gain.reshape(1, DIM), cosine[: 4 * ROWS], sine[: 4 * ROWS])

    store = [base] + [send(base, to_ring(s, 0)) for s in SHIFTS[1:]]
    store = jnp.concatenate(store, axis=0)
    store, q_mine = lax.optimization_barrier((store, q_mine))
    q_theirs = send(q_mine, to_core)
    arrived = [send(store, to_ring(s, 1)) for s in SHIFTS[1:3]]
    state_mine = attend(meta, q_mine, [store], None, False, (8,), 0)
    state_theirs = attend(meta, q_theirs, [store], None, False, (8,), 2)

    store, arrived, state_mine, state_theirs = lax.optimization_barrier(
        (store, arrived, state_mine, state_theirs)
    )
    last = send(store, to_ring(SHIFTS[3], 1))
    state_mine = attend(meta, q_mine, arrived, state_mine, False, (16, 24), 0)
    state_theirs = attend(meta, q_theirs, arrived, state_theirs, False, (16, 24), 2)
    last, state_mine, state_theirs = lax.optimization_barrier((last, state_mine, state_theirs))
    out_theirs = attend(meta, q_theirs, [last], state_theirs, True, (32,), 2)
    received = send(out_theirs, to_core)
    out_mine = attend(meta, q_mine, [last], state_mine, True, (32,), 0)

    joint = jax.ShapeDtypeStruct((TILE + STATS, DIM), jnp.bfloat16)
    parts = pl.pallas_call(
        join_kernel,
        in_specs=[VMEM] * 2,
        out_specs=[VMEM] * 4,
        out_shape=[joint] * 4,
        compiler_params=BIG,
    )(out_mine, received)
    home = [
        parts[0],
        send(parts[1], to_mate),
        send(parts[2], along_z(-2)),
        send(parts[3], along_z(-1)),
    ]

    return pl.pallas_call(
        finish_kernel,
        in_specs=[SMEM] + [VMEM] * 5,
        out_specs=VMEM,
        out_shape=jax.ShapeDtypeStruct(queries.shape, jnp.bfloat16),
        compiler_params=BIG,
    )(meta, *home, gate)


def solution(mesh):
    rows = P(("blk", "uly"), None)
    in_specs = (rows, rows, rows, rows, P(), P(), P())
    return jax.shard_map(local, mesh=mesh, in_specs=in_specs, out_specs=rows, check_vma=False)
```

```python
import functools

import jax
import jax.numpy as jnp
from jax import lax
from jax.experimental import pallas as pl
from jax.experimental.pallas import tpu as pltpu
from jax.sharding import PartitionSpec as P

ROTARY = 64
ROPE_BASE = 10000000.0
EPSILON = 1e-06
LOG2E = 1.4426950408889634

GRID = (4, 2, 2, 4, 4)
AXES = ("blk", "uly")
ROWS = 64
DIM = 256
GROUP = 8
TILE = GROUP * ROWS
STATS = 16
SPAN = 512
CHUNK = 128
SHIFTS = (0, 1, 3, 2)

HIDDEN = -1e30
EMPTY = -1e25


def place_of(index):
    place = []
    for extent in reversed(GRID):
        place.append(index % extent)
        index //= extent
    return tuple(reversed(place))


def index_of(place):
    index = 0
    for extent, at in zip(GRID, place):
        index = index * extent + at
    return index


def send(array, target):
    count = index_of(tuple(extent - 1 for extent in GRID)) + 1
    route = [(i, index_of(target(*place_of(i)))) for i in range(count)]
    return lax.ppermute(array, AXES, route)


def to_mate(x, zh, c, y, zl):
    return (x, zh, c, y, zl ^ 1)


def to_far(flip):
    return lambda x, zh, c, y, zl: (x, zh ^ 1, c, y, zl ^ flip)


def along_z(even):
    def target(x, zh, c, y, zl):
        z = (zh * 4 + zl + (-even if zl & 1 else even)) % 8
        return (x, z // 4, c, y, z % 4)

    return target


def to_core(x, zh, c, y, zl):
    return (x, zh, c ^ 1, y, zl)


def to_ring(shift, phase):
    def target(x, zh, c, y, zl):
        if c == phase:
            return ((x + shift) % 4, zh, c, y, zl)
        return (x, zh, c, (y + shift) % 4, zl)

    return target


def whole(*shape):
    return pl.BlockSpec(shape, lambda *_: (0,) * len(shape))


def turned(piece, gain, cosine, sine):
    piece = piece.astype(jnp.float32)
    scale = lax.rsqrt(jnp.mean(piece * piece, axis=-1, keepdims=True) + EPSILON)
    piece = piece * scale * gain
    front = piece[:, :128]
    lane = lax.broadcasted_iota(jnp.int32, front.shape, 1)
    half = ROTARY // 2
    partner = jnp.where(lane < half, pltpu.roll(front, 128 - half, 1), pltpu.roll(front, half, 1))
    front = front * cosine + partner * sine
    return jnp.concatenate([front, piece[:, 128:]], axis=-1).astype(jnp.bfloat16)


def split_kernel(place, keys, values, own, other):
    side = place[4] & 1
    for head, out in ((side, own), (1 - side, other)):
        columns = pl.ds(pl.multiple_of(head * DIM, DIM), DIM)
        out[:ROWS] = keys[:, columns]
        out[ROWS:] = values[:, columns]


def ring_source(at, shift):
    return (at + 4 - shift) & 3


def start_kernel(place, span_of, frequency, starts, angles):
    x, zh, c, y, zl = (place[n] for n in range(5))
    side = zl & 1

    def first_position(xs, zhs, cs, ys, within):
        slot = ((xs * 2 + zhs) * 2 + cs) * 2 + (ys >> 1)
        return span_of[slot] * SPAN + (ys & 1) * (SPAN // 2) + within

    z = zh * 4 + zl
    z_next = (z + jnp.where(side == 0, 7, 1)) & 7
    for core in range(2):
        for n, at in enumerate((z, z_next)):
            starts[2 * core + n] = first_position(
                x, at >> 2, c ^ core, y, ((at & 3) >> 1) * CHUNK
            )
    for a, outer in enumerate(SHIFTS):
        for b, inner in enumerate(SHIFTS):
            xs = jnp.where(c == 0, ring_source(x, inner), ring_source(x, outer))
            ys = jnp.where(c == 0, ring_source(y, outer), ring_source(y, inner))
            for t in range(2):
                starts[4 + a * 8 + b * 2 + t] = first_position(
                    xs, zh ^ t, c, ys, (zl >> 1) * CHUNK
                )
    row = lax.broadcasted_iota(jnp.int32, (ROWS, 128), 0)
    firsts = [starts[0] + side * ROWS]
    firsts += [starts[4 + t] + (side ^ n) * ROWS for t in range(2) for n in range(2)]
    for n, first in enumerate(firsts):
        angles[n * ROWS : (n + 1) * ROWS] = (row + first).astype(jnp.float32) * frequency[...]


STAGES = ((0, 8), (8, 16), (24, 8))
PER_TILE = 72
NEVER = -(1 << 20)


def plan_kernel(place, starts, q_gain, k_gain, plan):
    for tile in range(4):
        base = tile * PER_TILE

        def clear(n, carry):
            plan[base + n] = 0
            plan[base + 32 + n] = NEVER
            return carry

        lax.fori_loop(0, 32, clear, 0)
        for stage, (first, chunks) in enumerate(STAGES):

            def visit(j, count):
                reach = starts[tile] - starts[4 + first + j]
                seen = reach > -CHUNK
                at = base + first + count

                @pl.when(seen)
                def _():
                    plan[at] = j
                    plan[at + 32] = reach

                return count + seen.astype(jnp.int32)

            count = lax.fori_loop(0, chunks, visit, jnp.int32(0))
            plan[base + 64 + stage] = (count + 3) >> 2
    plan[4 * PER_TILE] = place[4] & 1
    bound = jnp.max(jnp.abs(q_gain[...])) * jnp.max(jnp.abs(k_gain[...])) * (16.0 * 1.02 * LOG2E)
    plan[4 * PER_TILE + 1] = (bound <= 100.0).astype(jnp.int32)


def keys_kernel(own, mate, far, cross, gain, cosine, sine, out):
    for n, piece in enumerate((own, mate, far, cross)):
        at = slice(n * ROWS, (n + 1) * ROWS)
        t, low = n // 2, (n % 2) * ROWS
        out[t, low : low + ROWS] = turned(piece[:ROWS], gain[...], cosine[at], sine[at])
        out[t, CHUNK + low : CHUNK + low + ROWS] = piece[ROWS:]


def queries_kernel(place, queries, gain, cosine, sine, own, other):
    side = place[4] & 1
    for head, out in ((side, own), (1 - side, other)):
        for member in range(GROUP):
            columns = pl.ds(pl.multiple_of((head * GROUP + member) * DIM, DIM), DIM)
            piece = turned(queries[:, columns], gain[...], cosine[...], sine[...])
            out[member * ROWS : (member + 1) * ROWS] = piece * jnp.bfloat16(DIM**-0.5)


def attend_kernel(stage, first_tile, buffers, plan, queries, *refs):
    first, last = stage == 0, stage == 2
    stores, refs = refs[:buffers], list(refs[buffers:])
    if not first:
        del refs[:3]
    if last:
        out = refs.pop(0)
    top, total, acc = refs
    side = plan[4 * PER_TILE]
    bounded = plan[4 * PER_TILE + 1] == 1
    per_store = stores[0].shape[0]
    bases = [(first_tile + tile) * PER_TILE for tile in range(2)]

    if first:
        top[...] = jnp.full(top.shape, jnp.where(bounded, 0.0, EMPTY), jnp.float32)
        total[...] = jnp.zeros(total.shape, jnp.float32)
        acc[...] = jnp.zeros(acc.shape, jnp.float32)

    def fetch(j, part):
        rows = slice(part * CHUNK, (part + 1) * CHUNK)
        if buffers == 1:
            return stores[0][j, rows]
        within = lax.rem(j, per_store)
        return jnp.where(j >= per_store, stores[1][within, rows], stores[0][within, rows])

    def absorb(plain, tile, n):
        at = bases[tile] + STAGES[stage][0] + 4 * n
        picks = [plan[at + m] for m in range(4)]
        limits = [plan[at + 32 + m] for m in range(4)]
        keys = jnp.concatenate([fetch(j, 0) for j in picks], axis=0)
        values = jnp.concatenate([fetch(j, 1) for j in picks], axis=0)
        for piece in range(2):
            rows = slice(piece * TILE, (piece + 1) * TILE)
            scores = lax.dot_general(
                queries[tile, rows],
                keys,
                (((1,), (1,)), ((), ())),
                preferred_element_type=jnp.float32,
            )
            scores = scores * LOG2E
            row = lax.broadcasted_iota(jnp.int32, (TILE, CHUNK), 0)
            lane = lax.broadcasted_iota(jnp.int32, (TILE, CHUNK), 1)
            gap = (lane ^ (side * ROWS)) - (row & (ROWS - 1)) - (side ^ piece) * ROWS
            parts = [
                jnp.where(gap <= limit, scores[:, m * CHUNK : (m + 1) * CHUNK], HIDDEN)
                for m, limit in enumerate(limits)
            ]
            if not plain:
                before = top[tile, rows]
                peak = functools.reduce(jnp.maximum, parts)
                now = jnp.maximum(before, jnp.max(peak, axis=-1, keepdims=True))
                fading = jnp.exp2(before - now)
                parts = [part - now for part in parts]
                top[tile, rows] = now
                total[tile, rows] = total[tile, rows] * fading
                acc[tile, rows] = acc[tile, rows] * jnp.concatenate([fading, fading], axis=-1)
            weights = [jnp.exp2(part) for part in parts]
            total[tile, rows] += functools.reduce(jnp.add, weights)
            acc[tile, rows] += jnp.dot(
                jnp.concatenate(weights, axis=-1).astype(jnp.bfloat16),
                values,
                preferred_element_type=jnp.float32,
            )

    steps = jnp.maximum(plan[bases[0] + 64 + stage], plan[bases[1] + 64 + stage])

    @pl.when(bounded)
    def _():
        def step(n, carry):
            absorb(True, 0, n)
            absorb(True, 1, n)
            return carry

        lax.fori_loop(0, steps, step, 0)

    @pl.when(jnp.logical_not(bounded))
    def _():
        def step(n, carry):
            absorb(False, 0, n)
            absorb(False, 1, n)
            return carry

        lax.fori_loop(0, steps, step, 0)

    if last:
        for tile in range(2):
            for piece in range(2):
                logs = []
                for sub in range(TILE // 128):
                    rows = slice(piece * TILE + sub * 128, piece * TILE + (sub + 1) * 128)
                    sums = jnp.sum(total[tile, rows], axis=-1, keepdims=True)
                    some = sums > 0.0
                    sums = jnp.where(some, sums, 1.0)
                    result = (acc[tile, rows] / sums).astype(jnp.bfloat16)
                    out[2 * tile + piece, sub * 128 : (sub + 1) * 128] = result
                    level = jnp.where(some, top[tile, rows] + jnp.log2(sums), EMPTY)
                    logs.append(level.T[:1])
                out[2 * tile + piece, TILE:] = packed(logs)


def packed(logs):
    level = jnp.concatenate(logs, axis=0)
    high = level.astype(jnp.bfloat16).astype(jnp.float32)
    middle = (level - high).astype(jnp.bfloat16).astype(jnp.float32)
    low = level - high - middle
    rows = jnp.concatenate([high, middle, low, jnp.zeros_like(low)], axis=0)
    return jnp.concatenate([rows, jnp.zeros_like(rows)], axis=-1).astype(jnp.bfloat16)


def unpacked(rows):
    rows = rows[:, :128].astype(jnp.float32)
    return rows[0:4] + rows[4:8] + rows[8:12]


def blend(left, right):
    a, b = unpacked(left), unpacked(right)
    peak = jnp.maximum(a, b)
    a, b = jnp.exp2(a - peak), jnp.exp2(b - peak)
    both = a + b
    return a / both, b / both, peak + jnp.log2(both)


def column(shares, n):
    share = jnp.broadcast_to(shares[n : n + 1], (128, 128)).T
    return jnp.concatenate([share, share], axis=-1)


def join_kernel(mine, theirs, *outs):
    for r, out in enumerate(outs):
        a, b, level = blend(mine[r, TILE:], theirs[r, TILE:])
        for n in range(TILE // 128):
            rows = slice(n * 128, (n + 1) * 128)
            left = mine[r, rows].astype(jnp.float32) * column(a, n)
            right = theirs[r, rows].astype(jnp.float32) * column(b, n)
            out[rows] = (left + right).astype(jnp.bfloat16)
        out[TILE:] = packed([level])


def finish_kernel(place, near0, near1, far0, far1, gate, out):
    side = place[4] & 1
    for which, (left_ref, right_ref) in enumerate(((near0, far0), (near1, far1))):
        head = side if which == 0 else 1 - side
        a, b, _ = blend(left_ref[TILE:], right_ref[TILE:])
        for n in range(TILE // 128):
            rows = slice(n * 128, (n + 1) * 128)
            left = left_ref[rows].astype(jnp.float32) * column(a, n)
            right = right_ref[rows].astype(jnp.float32) * column(b, n)
            attended = (left + right).astype(jnp.bfloat16).astype(jnp.float32)
            for m in range(2):
                at = (head * GROUP + 2 * n + m) * DIM
                columns = pl.ds(pl.multiple_of(at, DIM), DIM)
                logits = gate[:, columns].astype(jnp.float32)
                gated = attended[m * ROWS : (m + 1) * ROWS] * jax.nn.sigmoid(logits)
                out[:, columns] = gated.astype(jnp.bfloat16)


SMEM = pl.BlockSpec(memory_space=pltpu.SMEM)
VMEM = pl.BlockSpec(memory_space=pltpu.VMEM)
BIG = pltpu.CompilerParams(vmem_limit_bytes=28 * 1024 * 1024)


def attend(plan, queries, stores, state, stage, first_tile):
    shapes = [
        jax.ShapeDtypeStruct((2, 2 * TILE, width), jnp.float32) for width in (128, 128, DIM)
    ]
    if stage == 2:
        shapes = [jax.ShapeDtypeStruct((4, TILE + STATS, DIM), jnp.bfloat16)] + shapes
    given = 2 + len(stores)
    aliases = {given + n: n + (stage == 2) for n in range(len(state))}
    chunks = STAGES[stage][1]
    return pl.pallas_call(
        functools.partial(attend_kernel, stage, first_tile, len(stores)),
        in_specs=[SMEM] + [VMEM] * (1 + len(stores) + len(state)),
        out_specs=[VMEM] * len(shapes),
        out_shape=shapes,
        input_output_aliases=aliases,
        compiler_params=BIG,
        cost_estimate=pl.CostEstimate(
            flops=4 * 4 * TILE * chunks * CHUNK * DIM,
            bytes_accessed=4 << 20,
            transcendentals=4 * TILE * chunks * CHUNK,
        ),
    )(plan, queries, *stores, *state)


def local(queries, gate, keys, values, q_gain, k_gain, span_of):
    index = lax.axis_index("blk") * 16 + lax.axis_index("uly")
    place = jnp.stack(place_of(index)).astype(jnp.int32)
    q_gain, k_gain = q_gain.reshape(1, DIM), k_gain.reshape(1, DIM)

    pair = jax.ShapeDtypeStruct((2 * ROWS, DIM), jnp.bfloat16)
    kv_own, kv_other = pl.pallas_call(
        split_kernel,
        in_specs=[SMEM] + [VMEM] * 2,
        out_specs=[VMEM] * 2,
        out_shape=[pair, pair],
        compiler_params=BIG,
    )(place, keys, values)
    far = send(kv_own, to_far(0))
    cross = send(kv_other, to_far(1))
    mate = send(kv_other, to_mate)
    queries, span_of, _ = lax.optimization_barrier((queries, span_of, kv_own))

    lane = jnp.arange(128, dtype=jnp.int32)
    frequency = ROPE_BASE ** (-2.0 * (lane % 32).astype(jnp.float32) / ROTARY)
    starts, angles = pl.pallas_call(
        start_kernel,
        in_specs=[SMEM] * 2 + [VMEM],
        out_specs=[SMEM, VMEM],
        out_shape=[
            jax.ShapeDtypeStruct((36,), jnp.int32),
            jax.ShapeDtypeStruct((5 * ROWS, 128), jnp.float32),
        ],
        compiler_params=BIG,
    )(place, span_of, frequency.reshape(1, 128))
    rotated = lane[None, :] < ROTARY
    cosine = jnp.where(rotated, jnp.cos(angles), 1.0)
    sine = jnp.sin(angles)
    sine = jnp.where(rotated, jnp.where(lane[None, :] < ROTARY // 2, -sine, sine), 0.0)

    tile = jax.ShapeDtypeStruct((TILE, DIM), jnp.bfloat16)
    q_own, q_other = pl.pallas_call(
        queries_kernel,
        in_specs=[SMEM] + [VMEM] * 4,
        out_specs=[VMEM] * 2,
        out_shape=[tile, tile],
        compiler_params=BIG,
    )(place, queries, q_gain, cosine[:ROWS], sine[:ROWS])
    mate, far, cross, q_own, q_other = lax.optimization_barrier((mate, far, cross, q_own, q_other))

    base = pl.pallas_call(
        keys_kernel,
        in_specs=[VMEM] * 7,
        out_specs=VMEM,
        out_shape=jax.ShapeDtypeStruct((2, 2 * CHUNK, DIM), jnp.bfloat16),
        compiler_params=BIG,
    )(kv_own, mate, far, cross, k_gain, cosine[ROWS:], sine[ROWS:])

    plan = pl.pallas_call(
        plan_kernel,
        in_specs=[SMEM] * 2 + [VMEM] * 2,
        out_specs=SMEM,
        out_shape=jax.ShapeDtypeStruct((4 * PER_TILE + 8,), jnp.int32),
        compiler_params=BIG,
    )(place, starts, q_gain, k_gain)

    store = [base] + [send(base, to_ring(s, 0)) for s in SHIFTS[1:]]
    store = jnp.concatenate(store, axis=0)
    q_mine = jnp.stack(
        [q_own, send(q_other, to_mate), send(q_own, along_z(2)), send(q_other, along_z(-1))]
    ).reshape(2, 2 * TILE, DIM)
    store, q_mine = lax.optimization_barrier((store, q_mine))
    q_theirs = send(q_mine, to_core)
    arrived = [send(store, to_ring(s, 1)) for s in SHIFTS[1:3]]
    mine = attend(plan, q_mine, [store], [], 0, 0)
    theirs = attend(plan, q_theirs, [store], [], 0, 2)

    arrived, mine, theirs = lax.optimization_barrier((arrived, mine, theirs))
    last = [
        send(arrived[0][:4], to_ring(1, 1)),
        send(arrived[1][4:], to_ring(3, 1)),
    ]
    mine = attend(plan, q_mine, arrived, mine, 1, 0)
    theirs = attend(plan, q_theirs, arrived, theirs, 1, 2)
    last, mine, theirs = lax.optimization_barrier((last, mine, theirs))
    out_theirs = attend(plan, q_theirs, last, theirs, 2, 2)[0]
    received = send(out_theirs, to_core)
    out_mine = attend(plan, q_mine, last, mine, 2, 0)[0]

    joint = jax.ShapeDtypeStruct((TILE + STATS, DIM), jnp.bfloat16)
    parts = pl.pallas_call(
        join_kernel,
        in_specs=[VMEM] * 2,
        out_specs=[VMEM] * 4,
        out_shape=[joint] * 4,
        compiler_params=BIG,
    )(out_mine, received)
    home = [
        parts[0],
        send(parts[1], to_mate),
        send(parts[2], along_z(-2)),
        send(parts[3], along_z(-1)),
    ]

    return pl.pallas_call(
        finish_kernel,
        in_specs=[SMEM] + [VMEM] * 5,
        out_specs=VMEM,
        out_shape=jax.ShapeDtypeStruct(queries.shape, jnp.bfloat16),
        compiler_params=BIG,
    )(place, *home, gate)


def solution(mesh):
    rows = P(("blk", "uly"), None)
    in_specs = (rows, rows, rows, rows, P(), P(), P())
    return jax.shard_map(local, mesh=mesh, in_specs=in_specs, out_specs=rows, check_vma=False)
```

```python
import functools

import jax
import jax.numpy as jnp
from jax import lax
from jax.experimental import pallas as pl
from jax.experimental.pallas import tpu as pltpu
from jax.sharding import PartitionSpec as P

ROTARY = 64
ROPE_BASE = 10000000.0
EPSILON = 1e-06
LOG2E = 1.4426950408889634

GRID = (4, 2, 2, 4, 4)
AXES = ("blk", "uly")
ROWS = 64
DIM = 256
GROUP = 8
TILE = GROUP * ROWS
STATS = 16
SPAN = 512
CHUNK = 128
SHIFTS = (0, 1, 3, 2)

HIDDEN = -1e30
EMPTY = -1e25


def place_of(index):
    place = []
    for extent in reversed(GRID):
        place.append(index % extent)
        index //= extent
    return tuple(reversed(place))


def index_of(place):
    index = 0
    for extent, at in zip(GRID, place):
        index = index * extent + at
    return index


def send(array, target):
    count = index_of(tuple(extent - 1 for extent in GRID)) + 1
    route = [(i, index_of(target(*place_of(i)))) for i in range(count)]
    return lax.ppermute(array, AXES, route)


def to_mate(x, zh, c, y, zl):
    return (x, zh, c, y, zl ^ 1)


def to_far(flip):
    return lambda x, zh, c, y, zl: (x, zh ^ 1, c, y, zl ^ flip)


def along_z(even):
    def target(x, zh, c, y, zl):
        z = (zh * 4 + zl + (-even if zl & 1 else even)) % 8
        return (x, z // 4, c, y, z % 4)

    return target


def to_core(x, zh, c, y, zl):
    return (x, zh, c ^ 1, y, zl)


def to_ring(shift, phase):
    def target(x, zh, c, y, zl):
        if c == phase:
            return ((x + shift) % 4, zh, c, y, zl)
        return (x, zh, c, (y + shift) % 4, zl)

    return target


def whole(*shape):
    return pl.BlockSpec(shape, lambda *_: (0,) * len(shape))


def turned(piece, gain, cosine, sine):
    piece = piece.astype(jnp.float32)
    scale = lax.rsqrt(jnp.mean(piece * piece, axis=-1, keepdims=True) + EPSILON)
    piece = piece * scale * gain
    front = piece[:, :128]
    lane = lax.broadcasted_iota(jnp.int32, front.shape, 1)
    half = ROTARY // 2
    partner = jnp.where(lane < half, pltpu.roll(front, 128 - half, 1), pltpu.roll(front, half, 1))
    front = front * cosine + partner * sine
    return jnp.concatenate([front, piece[:, 128:]], axis=-1).astype(jnp.bfloat16)


def split_kernel(place, keys, values, own, other, done):
    side = place[4] & 1
    copies = []
    for n, (head, out) in enumerate(((side, own), (1 - side, other))):
        columns = pl.ds(pl.multiple_of(head * DIM, DIM), DIM)
        for m, source in enumerate((keys, values)):
            rows = pl.ds(m * ROWS, ROWS)
            copies.append(
                pltpu.make_async_copy(
                    source.at[:, columns], out.at[rows], done.at[2 * n + m]
                )
            )
    for copy in copies:
        copy.start()
    for copy in copies:
        copy.wait()


def ring_source(at, shift):
    return (at + 4 - shift) & 3


def start_kernel(place, span_of, frequency, starts, angles):
    x, zh, c, y, zl = (place[n] for n in range(5))
    side = zl & 1

    def first_position(xs, zhs, cs, ys, within):
        slot = ((xs * 2 + zhs) * 2 + cs) * 2 + (ys >> 1)
        return span_of[slot] * SPAN + (ys & 1) * (SPAN // 2) + within

    z = zh * 4 + zl
    z_next = (z + jnp.where(side == 0, 7, 1)) & 7
    for core in range(2):
        for n, at in enumerate((z, z_next)):
            starts[2 * core + n] = first_position(
                x, at >> 2, c ^ core, y, ((at & 3) >> 1) * CHUNK
            )
    for a, outer in enumerate(SHIFTS):
        for b, inner in enumerate(SHIFTS):
            xs = jnp.where(c == 0, ring_source(x, inner), ring_source(x, outer))
            ys = jnp.where(c == 0, ring_source(y, outer), ring_source(y, inner))
            for t in range(2):
                starts[4 + a * 8 + b * 2 + t] = first_position(
                    xs, zh ^ t, c, ys, (zl >> 1) * CHUNK
                )
    row = lax.broadcasted_iota(jnp.int32, (ROWS, 128), 0)
    firsts = [starts[0] + side * ROWS]
    firsts += [starts[4 + t] + (side ^ n) * ROWS for t in range(2) for n in range(2)]
    for n, first in enumerate(firsts):
        angles[n * ROWS : (n + 1) * ROWS] = (row + first).astype(jnp.float32) * frequency[...]


STAGES = ((0, 8), (8, 16), (24, 8))
PER_TILE = 72
NEVER = -(1 << 20)


def plan_kernel(place, starts, q_gain, k_gain, plan):
    for tile in range(4):
        base = tile * PER_TILE

        def clear(n, carry):
            plan[base + n] = 0
            plan[base + 32 + n] = NEVER
            return carry

        lax.fori_loop(0, 32, clear, 0)
        for stage, (first, chunks) in enumerate(STAGES):

            def visit(j, count):
                reach = starts[tile] - starts[4 + first + j]
                seen = reach > -CHUNK
                at = base + first + count

                @pl.when(seen)
                def _():
                    plan[at] = j
                    plan[at + 32] = reach

                return count + seen.astype(jnp.int32)

            count = lax.fori_loop(0, chunks, visit, jnp.int32(0))
            plan[base + 64 + stage] = (count + 3) >> 2
    plan[4 * PER_TILE] = place[4] & 1
    bound = jnp.max(jnp.abs(q_gain[...])) * jnp.max(jnp.abs(k_gain[...])) * (16.0 * 1.02 * LOG2E)
    plan[4 * PER_TILE + 1] = (bound <= 100.0).astype(jnp.int32)


def keys_kernel(own, mate, far, cross, gain, cosine, sine, out):
    for n, piece in enumerate((own, mate, far, cross)):
        at = slice(n * ROWS, (n + 1) * ROWS)
        t, low = n // 2, (n % 2) * ROWS
        out[t, low : low + ROWS] = turned(piece[:ROWS], gain[...], cosine[at], sine[at])
        out[t, CHUNK + low : CHUNK + low + ROWS] = piece[ROWS:]


def queries_kernel(place, queries, gain, cosine, sine, own, other):
    side = place[4] & 1
    for head, out in ((side, own), (1 - side, other)):
        for member in range(GROUP):
            columns = pl.ds(pl.multiple_of((head * GROUP + member) * DIM, DIM), DIM)
            piece = turned(queries[:, columns], gain[...], cosine[...], sine[...])
            out[member * ROWS : (member + 1) * ROWS] = piece * jnp.bfloat16(DIM**-0.5)


def attend_kernel(stage, first_tile, buffers, plan, queries, *refs):
    first, last = stage == 0, stage == 2
    stores, refs = refs[:buffers], list(refs[buffers:])
    if not first:
        del refs[:3]
    if last:
        out = refs.pop(0)
    top, total, acc = refs
    side = plan[4 * PER_TILE]
    bounded = plan[4 * PER_TILE + 1] == 1
    per_store = stores[0].shape[0]

    if first:
        top[...] = jnp.full(top.shape, jnp.where(bounded, 0.0, EMPTY), jnp.float32)
        total[...] = jnp.zeros(total.shape, jnp.float32)
        acc[...] = jnp.zeros(acc.shape, jnp.float32)

    def fetch(j, part):
        rows = slice(part * CHUNK, (part + 1) * CHUNK)
        if buffers == 1:
            return stores[0][j, rows]
        within = lax.rem(j, per_store)
        return jnp.where(j >= per_store, stores[1][within, rows], stores[0][within, rows])

    row = lax.broadcasted_iota(jnp.int32, (TILE, CHUNK), 0)
    lane = lax.broadcasted_iota(jnp.int32, (TILE, CHUNK), 1)

    def gather(tile, n):
        at = (first_tile + tile) * PER_TILE + STAGES[stage][0] + 4 * n
        picks = [plan[at + m] for m in range(4)]
        limits = [plan[at + 32 + m] for m in range(4)]
        keys = jnp.concatenate([fetch(j, 0) for j in picks], axis=0)
        values = jnp.concatenate([fetch(j, 1) for j in picks], axis=0)
        return keys, values, limits

    def scores_of(tile, piece, rows, keys, limits):
        scores = lax.dot_general(
            queries[tile, rows],
            keys,
            (((1,), (1,)), ((), ())),
            preferred_element_type=jnp.float32,
        )
        scores = scores * LOG2E
        gap = (lane ^ (side * ROWS)) - (row & (ROWS - 1)) - (side ^ piece) * ROWS
        return [
            jnp.where(gap <= limit, scores[:, m * CHUNK : (m + 1) * CHUNK], HIDDEN)
            for m, limit in enumerate(limits)
        ]

    def add(tile, rows, parts, values):
        weights = [jnp.exp2(part) for part in parts]
        total[tile, rows] += functools.reduce(jnp.add, weights)
        acc[tile, rows] += jnp.dot(
            jnp.concatenate(weights, axis=-1).astype(jnp.bfloat16),
            values,
            preferred_element_type=jnp.float32,
        )

    bases = [(first_tile + tile) * PER_TILE for tile in range(2)]
    steps = jnp.maximum(plan[bases[0] + 64 + stage], plan[bases[1] + 64 + stage])

    @pl.when(bounded)
    def _():
        def step(n, carry):
            for tile in range(2):
                keys, values, limits = gather(tile, n)
                for piece in range(2):
                    rows = slice(piece * TILE, (piece + 1) * TILE)
                    add(tile, rows, scores_of(tile, piece, rows, keys, limits), values)
            return carry

        lax.fori_loop(0, steps, step, 0)

    @pl.when(jnp.logical_not(bounded))
    def _():
        def step(n, carry):
            tile, piece = (n >> 1) & 1, n & 1
            keys, values, limits = gather(tile, n >> 2)
            rows = pl.ds(pl.multiple_of(piece * TILE, TILE), TILE)
            parts = scores_of(tile, piece, rows, keys, limits)
            before = top[tile, rows]
            peak = functools.reduce(jnp.maximum, parts)
            now = jnp.maximum(before, jnp.max(peak, axis=-1, keepdims=True))
            fading = jnp.exp2(before - now)
            top[tile, rows] = now
            total[tile, rows] = total[tile, rows] * fading
            acc[tile, rows] = acc[tile, rows] * jnp.concatenate([fading, fading], axis=-1)
            add(tile, rows, [part - now for part in parts], values)
            return carry

        lax.fori_loop(0, 4 * steps, step, 0)

    if last:
        for tile in range(2):
            for piece in range(2):
                logs = []
                for sub in range(TILE // 128):
                    rows = slice(piece * TILE + sub * 128, piece * TILE + (sub + 1) * 128)
                    sums = jnp.sum(total[tile, rows], axis=-1, keepdims=True)
                    some = sums > 0.0
                    sums = jnp.where(some, sums, 1.0)
                    result = (acc[tile, rows] / sums).astype(jnp.bfloat16)
                    out[2 * tile + piece, sub * 128 : (sub + 1) * 128] = result
                    level = jnp.where(some, top[tile, rows] + jnp.log2(sums), EMPTY)
                    logs.append(level.T[:1])
                out[2 * tile + piece, TILE:] = packed(logs)


def packed(logs):
    level = jnp.concatenate(logs, axis=0)
    high = level.astype(jnp.bfloat16).astype(jnp.float32)
    middle = (level - high).astype(jnp.bfloat16).astype(jnp.float32)
    low = level - high - middle
    rows = jnp.concatenate([high, middle, low, jnp.zeros_like(low)], axis=0)
    return jnp.concatenate([rows, jnp.zeros_like(rows)], axis=-1).astype(jnp.bfloat16)


def unpacked(rows):
    rows = rows[:, :128].astype(jnp.float32)
    return rows[0:4] + rows[4:8] + rows[8:12]


def blend(left, right):
    a, b = unpacked(left), unpacked(right)
    peak = jnp.maximum(a, b)
    a, b = jnp.exp2(a - peak), jnp.exp2(b - peak)
    both = a + b
    return a / both, b / both, peak + jnp.log2(both)


def column(shares, n):
    share = jnp.broadcast_to(shares[n : n + 1], (128, 128)).T
    return jnp.concatenate([share, share], axis=-1)


def join_kernel(mine, theirs, *outs):
    for r, out in enumerate(outs):
        a, b, level = blend(mine[r, TILE:], theirs[r, TILE:])
        for n in range(TILE // 128):
            rows = slice(n * 128, (n + 1) * 128)
            left = mine[r, rows].astype(jnp.float32) * column(a, n)
            right = theirs[r, rows].astype(jnp.float32) * column(b, n)
            out[rows] = (left + right).astype(jnp.bfloat16)
        out[TILE:] = packed([level])


def finish_kernel(place, near0, near1, far0, far1, gate, out):
    side = place[4] & 1
    for which, (left_ref, right_ref) in enumerate(((near0, far0), (near1, far1))):
        head = side if which == 0 else 1 - side
        a, b, _ = blend(left_ref[TILE:], right_ref[TILE:])
        for n in range(TILE // 128):
            rows = slice(n * 128, (n + 1) * 128)
            left = left_ref[rows].astype(jnp.float32) * column(a, n)
            right = right_ref[rows].astype(jnp.float32) * column(b, n)
            attended = (left + right).astype(jnp.bfloat16).astype(jnp.float32)
            for m in range(2):
                at = (head * GROUP + 2 * n + m) * DIM
                columns = pl.ds(pl.multiple_of(at, DIM), DIM)
                logits = gate[:, columns].astype(jnp.float32)
                gated = attended[m * ROWS : (m + 1) * ROWS] * jax.nn.sigmoid(logits)
                out[:, columns] = gated.astype(jnp.bfloat16)


SMEM = pl.BlockSpec(memory_space=pltpu.SMEM)
VMEM = pl.BlockSpec(memory_space=pltpu.VMEM)
BIG = pltpu.CompilerParams(vmem_limit_bytes=28 * 1024 * 1024)


def attend(plan, queries, stores, state, stage, first_tile):
    shapes = [
        jax.ShapeDtypeStruct((2, 2 * TILE, width), jnp.float32) for width in (128, 128, DIM)
    ]
    if stage == 2:
        shapes = [jax.ShapeDtypeStruct((4, TILE + STATS, DIM), jnp.bfloat16)] + shapes
    given = 2 + len(stores)
    aliases = {given + n: n + (stage == 2) for n in range(len(state))}
    chunks = STAGES[stage][1]
    return pl.pallas_call(
        functools.partial(attend_kernel, stage, first_tile, len(stores)),
        in_specs=[SMEM] + [VMEM] * (1 + len(stores) + len(state)),
        out_specs=[VMEM] * len(shapes),
        out_shape=shapes,
        input_output_aliases=aliases,
        compiler_params=BIG,
        cost_estimate=pl.CostEstimate(
            flops=4 * 4 * TILE * chunks * CHUNK * DIM,
            bytes_accessed=4 << 20,
            transcendentals=4 * TILE * chunks * CHUNK,
        ),
    )(plan, queries, *stores, *state)


def local(queries, gate, keys, values, q_gain, k_gain, span_of):
    index = lax.axis_index("blk") * 16 + lax.axis_index("uly")
    place = jnp.stack(place_of(index)).astype(jnp.int32)
    q_gain, k_gain = q_gain.reshape(1, DIM), k_gain.reshape(1, DIM)

    pair = jax.ShapeDtypeStruct((2 * ROWS, DIM), jnp.bfloat16)
    kv_own, kv_other = pl.pallas_call(
        split_kernel,
        in_specs=[SMEM] + [pl.BlockSpec(memory_space=pl.ANY)] * 2,
        out_specs=[VMEM] * 2,
        out_shape=[pair, pair],
        scratch_shapes=[pltpu.SemaphoreType.DMA((4,))],
        compiler_params=BIG,
    )(place, keys, values)
    far = send(kv_own, to_far(0))
    cross = send(kv_other, to_far(1))
    mate = send(kv_other, to_mate)
    span_of, _ = lax.optimization_barrier((span_of, kv_own))

    lane = jnp.arange(128, dtype=jnp.int32)
    frequency = ROPE_BASE ** (-2.0 * (lane % 32).astype(jnp.float32) / ROTARY)
    starts, angles = pl.pallas_call(
        start_kernel,
        in_specs=[SMEM] * 2 + [VMEM],
        out_specs=[SMEM, VMEM],
        out_shape=[
            jax.ShapeDtypeStruct((36,), jnp.int32),
            jax.ShapeDtypeStruct((5 * ROWS, 128), jnp.float32),
        ],
        compiler_params=BIG,
    )(place, span_of, frequency.reshape(1, 128))
    rotated = lane[None, :] < ROTARY
    cosine = jnp.where(rotated, jnp.cos(angles), 1.0)
    sine = jnp.sin(angles)
    sine = jnp.where(rotated, jnp.where(lane[None, :] < ROTARY // 2, -sine, sine), 0.0)

    tile = jax.ShapeDtypeStruct((TILE, DIM), jnp.bfloat16)
    q_own, q_other = pl.pallas_call(
        queries_kernel,
        in_specs=[SMEM] + [VMEM] * 4,
        out_specs=[VMEM] * 2,
        out_shape=[tile, tile],
        compiler_params=BIG,
    )(place, queries, q_gain, cosine[:ROWS], sine[:ROWS])
    mate, far, cross, q_own, q_other = lax.optimization_barrier((mate, far, cross, q_own, q_other))

    base = pl.pallas_call(
        keys_kernel,
        in_specs=[VMEM] * 7,
        out_specs=VMEM,
        out_shape=jax.ShapeDtypeStruct((2, 2 * CHUNK, DIM), jnp.bfloat16),
        compiler_params=BIG,
    )(kv_own, mate, far, cross, k_gain, cosine[ROWS:], sine[ROWS:])

    plan = pl.pallas_call(
        plan_kernel,
        in_specs=[SMEM] * 2 + [VMEM] * 2,
        out_specs=SMEM,
        out_shape=jax.ShapeDtypeStruct((4 * PER_TILE + 8,), jnp.int32),
        compiler_params=BIG,
    )(place, starts, q_gain, k_gain)

    store = [base] + [send(base, to_ring(s, 0)) for s in SHIFTS[1:]]
    store = jnp.concatenate(store, axis=0)
    q_mine = jnp.stack(
        [q_own, send(q_other, to_mate), send(q_own, along_z(2)), send(q_other, along_z(-1))]
    ).reshape(2, 2 * TILE, DIM)
    store, q_mine, plan = lax.optimization_barrier((store, q_mine, plan))
    q_theirs = send(q_mine, to_core)
    arrived = [send(store, to_ring(s, 1)) for s in SHIFTS[1:3]]
    mine = attend(plan, q_mine, [store], [], 0, 0)
    theirs = attend(plan, q_theirs, [store], [], 0, 2)

    arrived, mine, theirs = lax.optimization_barrier((arrived, mine, theirs))
    last = [
        send(arrived[0][:4], to_ring(1, 1)),
        send(arrived[1][4:], to_ring(3, 1)),
    ]
    mine = attend(plan, q_mine, arrived, mine, 1, 0)
    theirs = attend(plan, q_theirs, arrived, theirs, 1, 2)
    last, mine, theirs = lax.optimization_barrier((last, mine, theirs))
    out_theirs = attend(plan, q_theirs, last, theirs, 2, 2)[0]
    received = send(out_theirs, to_core)
    out_mine = attend(plan, q_mine, last, mine, 2, 0)[0]

    joint = jax.ShapeDtypeStruct((TILE + STATS, DIM), jnp.bfloat16)
    parts = pl.pallas_call(
        join_kernel,
        in_specs=[VMEM] * 2,
        out_specs=[VMEM] * 4,
        out_shape=[joint] * 4,
        compiler_params=BIG,
    )(out_mine, received)
    home = [
        parts[0],
        send(parts[1], to_mate),
        send(parts[2], along_z(-2)),
        send(parts[3], along_z(-1)),
    ]

    return pl.pallas_call(
        finish_kernel,
        in_specs=[SMEM] + [VMEM] * 5,
        out_specs=VMEM,
        out_shape=jax.ShapeDtypeStruct(queries.shape, jnp.bfloat16),
        compiler_params=BIG,
    )(place, *home, gate)


def solution(mesh):
    rows = P(("blk", "uly"), None)
    in_specs = (rows, rows, rows, rows, P(), P(), P())
    return jax.shard_map(local, mesh=mesh, in_specs=in_specs, out_specs=rows, check_vma=False)
```

```python
import functools

import jax
import jax.numpy as jnp
from jax import lax
from jax.experimental import pallas as pl
from jax.experimental.pallas import tpu as pltpu
from jax.sharding import PartitionSpec as P

ROTARY = 64
ROPE_BASE = 10000000.0
EPSILON = 1e-06
LOG2E = 1.4426950408889634

GRID = (4, 2, 2, 4, 4)
AXES = ("blk", "uly")
ROWS = 64
DIM = 256
GROUP = 8
TILE = GROUP * ROWS
STATS = 16
SPAN = 512
CHUNK = 128
SHIFTS = (0, 1, 3, 2)

HIDDEN = -1e30
EMPTY = -1e25


def place_of(index):
    place = []
    for extent in reversed(GRID):
        place.append(index % extent)
        index //= extent
    return tuple(reversed(place))


def index_of(place):
    index = 0
    for extent, at in zip(GRID, place):
        index = index * extent + at
    return index


def send(array, target):
    count = index_of(tuple(extent - 1 for extent in GRID)) + 1
    route = [(i, index_of(target(*place_of(i)))) for i in range(count)]
    return lax.ppermute(array, AXES, route)


def to_mate(x, zh, c, y, zl):
    return (x, zh, c, y, zl ^ 1)


def to_far(flip):
    return lambda x, zh, c, y, zl: (x, zh ^ 1, c, y, zl ^ flip)


def along_z(even):
    def target(x, zh, c, y, zl):
        z = (zh * 4 + zl + (-even if zl & 1 else even)) % 8
        return (x, z // 4, c, y, z % 4)

    return target


def to_core(x, zh, c, y, zl):
    return (x, zh, c ^ 1, y, zl)


def to_ring(shift, phase):
    def target(x, zh, c, y, zl):
        if c == phase:
            return ((x + shift) % 4, zh, c, y, zl)
        return (x, zh, c, (y + shift) % 4, zl)

    return target


def whole(*shape):
    return pl.BlockSpec(shape, lambda *_: (0,) * len(shape))


def turned(piece, gain, cosine, sine):
    piece = piece.astype(jnp.float32)
    scale = lax.rsqrt(jnp.mean(piece * piece, axis=-1, keepdims=True) + EPSILON)
    piece = piece * scale * gain
    front = piece[:, :128]
    lane = lax.broadcasted_iota(jnp.int32, front.shape, 1)
    half = ROTARY // 2
    partner = jnp.where(lane < half, pltpu.roll(front, 128 - half, 1), pltpu.roll(front, half, 1))
    front = front * cosine + partner * sine
    return jnp.concatenate([front, piece[:, 128:]], axis=-1).astype(jnp.bfloat16)


def split_kernel(place, keys, values, own, other, done):
    side = place[4] & 1
    copies = []
    for n, (head, out) in enumerate(((side, own), (1 - side, other))):
        columns = pl.ds(pl.multiple_of(head * DIM, DIM), DIM)
        for m, source in enumerate((keys, values)):
            rows = pl.ds(m * ROWS, ROWS)
            copies.append(
                pltpu.make_async_copy(
                    source.at[:, columns], out.at[rows], done.at[2 * n + m]
                )
            )
    for copy in copies:
        copy.start()
    for copy in copies:
        copy.wait()


def ring_source(at, shift):
    return (at + 4 - shift) & 3


STAGES = ((0, 8), (8, 8), (16, 8), (24, 8))
PER_TILE = 72
NEVER = -(1 << 20)

ORDER = ((0, 0), (0, 4), (1, 0), (3, 4), (1, 4), (3, 0), (2, 0), (2, 4))


def prepare_kernel(
    place,
    span_of,
    frequency,
    gain,
    k_gain,
    queries,
    plan,
    cosine,
    sine,
    own,
    other,
    starts,
    fetched,
    done,
):
    fetch = pltpu.make_async_copy(queries, fetched, done.at[0])
    fetch.start()
    x, zh, c, y, zl = (place[n] for n in range(5))
    side = zl & 1

    def first_position(xs, zhs, cs, ys, within):
        slot = ((xs * 2 + zhs) * 2 + cs) * 2 + (ys >> 1)
        return span_of[slot] * SPAN + (ys & 1) * (SPAN // 2) + within

    z = zh * 4 + zl
    z_next = (z + jnp.where(side == 0, 7, 1)) & 7
    for core in range(2):
        for n, at in enumerate((z, z_next)):
            starts[2 * core + n] = first_position(
                x, at >> 2, c ^ core, y, ((at & 3) >> 1) * CHUNK
            )
    for a, (outer, low) in enumerate(ORDER):
        for b in range(4):
            inner = SHIFTS[(low + b) // 2]
            xs = jnp.where(c == 0, ring_source(x, inner), ring_source(x, outer))
            ys = jnp.where(c == 0, ring_source(y, outer), ring_source(y, inner))
            starts[4 + a * 4 + b] = first_position(
                xs, zh ^ (b & 1), c, ys, (zl >> 1) * CHUNK
            )

    row = lax.broadcasted_iota(jnp.int32, (ROWS, 128), 0)
    lane = lax.broadcasted_iota(jnp.int32, (ROWS, 128), 1)

    def rotation(first):
        angles = (row + first).astype(jnp.float32) * frequency[...]
        sines = jnp.sin(angles)
        sines = jnp.where(lane < ROTARY // 2, -sines, sines)
        rotated = lane < ROTARY
        return jnp.where(rotated, jnp.cos(angles), 1.0), jnp.where(rotated, sines, 0.0)

    for t in range(2):
        for n in range(2):
            rows = slice((2 * t + n) * ROWS, (2 * t + n + 1) * ROWS)
            cosine[rows], sine[rows] = rotation(starts[4 + t] + (side ^ n) * ROWS)
    q_cosine, q_sine = rotation(starts[0] + side * ROWS)
    fetch.wait()
    for head, out in ((side, own), (1 - side, other)):
        for member in range(GROUP):
            columns = pl.ds(pl.multiple_of((head * GROUP + member) * DIM, DIM), DIM)
            piece = turned(fetched[:, columns], gain[...], q_cosine, q_sine)
            out[member * ROWS : (member + 1) * ROWS] = piece * jnp.bfloat16(DIM**-0.5)

    for t in range(4):
        for stage, (first, chunks) in enumerate(STAGES):
            at = t * PER_TILE + first
            count = jnp.int32(0)
            for j in range(chunks):
                reach = starts[t] - starts[4 + first + j]
                plan[at + count] = j
                plan[at + 32 + count] = reach
                count += (reach > -CHUNK).astype(jnp.int32)
            plan[t * PER_TILE + 64 + stage] = count
    plan[4 * PER_TILE] = side
    bound = jnp.max(jnp.abs(gain[...])) * jnp.max(jnp.abs(k_gain[...])) * (16.0 * 1.02 * LOG2E)
    plan[4 * PER_TILE + 1] = (bound <= 100.0).astype(jnp.int32)


def keys_kernel(own, mate, far, cross, gain, cosine, sine, out):
    for n, piece in enumerate((own, mate, far, cross)):
        at = slice(n * ROWS, (n + 1) * ROWS)
        t, low = n // 2, (n % 2) * ROWS
        out[t, low : low + ROWS] = turned(piece[:ROWS], gain[...], cosine[at], sine[at])
        out[t, CHUNK + low : CHUNK + low + ROWS] = piece[ROWS:]


def attend_kernel(stage, first_tile, buffers, plan, queries, *refs):
    first, last = stage == 0, stage == 3
    stores, refs = refs[:buffers], list(refs[buffers:])
    if not first:
        del refs[:3]
    if last:
        out = refs.pop(0)
    top, total, acc = refs
    side = plan[4 * PER_TILE]
    bounded = plan[4 * PER_TILE + 1] == 1
    per_store = stores[0].shape[0]

    if first:
        top[...] = jnp.full(top.shape, jnp.where(bounded, 0.0, EMPTY), jnp.float32)
        total[...] = jnp.zeros(total.shape, jnp.float32)
        acc[...] = jnp.zeros(acc.shape, jnp.float32)

    def fetch(j, part):
        rows = slice(part * CHUNK, (part + 1) * CHUNK)
        within = lax.rem(j, per_store)
        picked = stores[0][within, rows]
        for n in range(1, buffers):
            picked = jnp.where(j >= n * per_store, stores[n][within, rows], picked)
        return picked

    row = lax.broadcasted_iota(jnp.int32, (TILE, CHUNK), 0)
    lane = lax.broadcasted_iota(jnp.int32, (TILE, CHUNK), 1)

    def gather(tile, n):
        base = (first_tile + tile) * PER_TILE
        at = base + STAGES[stage][0] + 4 * n
        real = [4 * n + m < plan[base + 64 + stage] for m in range(4)]
        picks = [jnp.where(real[m], plan[at + m], 0) for m in range(4)]
        limits = [jnp.where(real[m], plan[at + 32 + m], NEVER) for m in range(4)]
        keys = jnp.concatenate([fetch(j, 0) for j in picks], axis=0)
        values = jnp.concatenate([fetch(j, 1) for j in picks], axis=0)
        return keys, values, limits

    def scores_of(tile, piece, rows, keys, limits):
        scores = lax.dot_general(
            queries[tile, rows],
            keys,
            (((1,), (1,)), ((), ())),
            preferred_element_type=jnp.float32,
        )
        scores = scores * LOG2E
        gap = (lane ^ (side * ROWS)) - (row & (ROWS - 1)) - (side ^ piece) * ROWS
        return [
            jnp.where(gap <= limit, scores[:, m * CHUNK : (m + 1) * CHUNK], HIDDEN)
            for m, limit in enumerate(limits)
        ]

    def add(tile, rows, parts, values):
        weights = [jnp.exp2(part) for part in parts]
        total[tile, rows] += functools.reduce(jnp.add, weights)
        acc[tile, rows] += jnp.dot(
            jnp.concatenate(weights, axis=-1).astype(jnp.bfloat16),
            values,
            preferred_element_type=jnp.float32,
        )

    bases = [(first_tile + tile) * PER_TILE for tile in range(2)]
    steps = (jnp.maximum(plan[bases[0] + 64 + stage], plan[bases[1] + 64 + stage]) + 3) >> 2

    @pl.when(bounded)
    def _():
        def step(n, carry):
            for tile in range(2):
                keys, values, limits = gather(tile, n)
                for piece in range(2):
                    rows = slice(piece * TILE, (piece + 1) * TILE)
                    add(tile, rows, scores_of(tile, piece, rows, keys, limits), values)
            return carry

        lax.fori_loop(0, steps, step, 0)

    @pl.when(jnp.logical_not(bounded))
    def _():
        def step(n, carry):
            tile, piece = (n >> 1) & 1, n & 1
            keys, values, limits = gather(tile, n >> 2)
            rows = pl.ds(pl.multiple_of(piece * TILE, TILE), TILE)
            parts = scores_of(tile, piece, rows, keys, limits)
            before = top[tile, rows]
            peak = functools.reduce(jnp.maximum, parts)
            now = jnp.maximum(before, jnp.max(peak, axis=-1, keepdims=True))
            fading = jnp.exp2(before - now)
            top[tile, rows] = now
            total[tile, rows] = total[tile, rows] * fading
            acc[tile, rows] = acc[tile, rows] * jnp.concatenate([fading, fading], axis=-1)
            add(tile, rows, [part - now for part in parts], values)
            return carry

        lax.fori_loop(0, 4 * steps, step, 0)

    if last:
        for tile in range(2):
            for piece in range(2):
                logs = []
                for sub in range(TILE // 128):
                    rows = slice(piece * TILE + sub * 128, piece * TILE + (sub + 1) * 128)
                    sums = jnp.sum(total[tile, rows], axis=-1, keepdims=True)
                    some = sums > 0.0
                    sums = jnp.where(some, sums, 1.0)
                    result = (acc[tile, rows] / sums).astype(jnp.bfloat16)
                    out[2 * tile + piece, sub * 128 : (sub + 1) * 128] = result
                    level = jnp.where(some, top[tile, rows] + jnp.log2(sums), EMPTY)
                    logs.append(level.T[:1])
                out[2 * tile + piece, TILE:] = packed(logs)


def packed(logs):
    level = jnp.concatenate(logs, axis=0)
    high = level.astype(jnp.bfloat16).astype(jnp.float32)
    middle = (level - high).astype(jnp.bfloat16).astype(jnp.float32)
    low = level - high - middle
    rows = jnp.concatenate([high, middle, low, jnp.zeros_like(low)], axis=0)
    return jnp.concatenate([rows, jnp.zeros_like(rows)], axis=-1).astype(jnp.bfloat16)


def unpacked(rows):
    rows = rows[:, :128].astype(jnp.float32)
    return rows[0:4] + rows[4:8] + rows[8:12]


def blend(left, right):
    a, b = unpacked(left), unpacked(right)
    peak = jnp.maximum(a, b)
    a, b = jnp.exp2(a - peak), jnp.exp2(b - peak)
    both = a + b
    return a / both, b / both, peak + jnp.log2(both)


def column(shares, n):
    share = jnp.broadcast_to(shares[n : n + 1], (128, 128)).T
    return jnp.concatenate([share, share], axis=-1)


def join_kernel(mine, theirs, *outs):
    for r, out in enumerate(outs):
        a, b, level = blend(mine[r, TILE:], theirs[r, TILE:])
        for n in range(TILE // 128):
            rows = slice(n * 128, (n + 1) * 128)
            left = mine[r, rows].astype(jnp.float32) * column(a, n)
            right = theirs[r, rows].astype(jnp.float32) * column(b, n)
            out[rows] = (left + right).astype(jnp.bfloat16)
        out[TILE:] = packed([level])


def finish_kernel(place, near0, near1, far0, far1, gate, out):
    side = place[4] & 1
    for which, (left_ref, right_ref) in enumerate(((near0, far0), (near1, far1))):
        head = side if which == 0 else 1 - side
        a, b, _ = blend(left_ref[TILE:], right_ref[TILE:])
        for n in range(TILE // 128):
            rows = slice(n * 128, (n + 1) * 128)
            left = left_ref[rows].astype(jnp.float32) * column(a, n)
            right = right_ref[rows].astype(jnp.float32) * column(b, n)
            attended = (left + right).astype(jnp.bfloat16).astype(jnp.float32)
            for m in range(2):
                at = (head * GROUP + 2 * n + m) * DIM
                columns = pl.ds(pl.multiple_of(at, DIM), DIM)
                logits = gate[:, columns].astype(jnp.float32)
                gated = attended[m * ROWS : (m + 1) * ROWS] * jax.nn.sigmoid(logits)
                out[:, columns] = gated.astype(jnp.bfloat16)


SMEM = pl.BlockSpec(memory_space=pltpu.SMEM)
VMEM = pl.BlockSpec(memory_space=pltpu.VMEM)
BIG = pltpu.CompilerParams(vmem_limit_bytes=28 * 1024 * 1024)


def attend(plan, queries, stores, state, stage, first_tile):
    shapes = [
        jax.ShapeDtypeStruct((2, 2 * TILE, width), jnp.float32) for width in (128, 128, DIM)
    ]
    if stage == 3:
        shapes = [jax.ShapeDtypeStruct((4, TILE + STATS, DIM), jnp.bfloat16)] + shapes
    given = 2 + len(stores)
    aliases = {given + n: n + (stage == 3) for n in range(len(state))}
    chunks = STAGES[stage][1]
    return pl.pallas_call(
        functools.partial(attend_kernel, stage, first_tile, len(stores)),
        in_specs=[SMEM] + [VMEM] * (1 + len(stores) + len(state)),
        out_specs=[VMEM] * len(shapes),
        out_shape=shapes,
        input_output_aliases=aliases,
        compiler_params=BIG,
        cost_estimate=pl.CostEstimate(
            flops=4 * 4 * TILE * chunks * CHUNK * DIM,
            bytes_accessed=4 << 20,
            transcendentals=4 * TILE * chunks * CHUNK,
        ),
    )(plan, queries, *stores, *state)


def local(queries, gate, keys, values, q_gain, k_gain, span_of):
    index = lax.axis_index("blk") * 16 + lax.axis_index("uly")
    place = jnp.stack(place_of(index)).astype(jnp.int32)
    q_gain, k_gain = q_gain.reshape(1, DIM), k_gain.reshape(1, DIM)

    pair = jax.ShapeDtypeStruct((2 * ROWS, DIM), jnp.bfloat16)
    kv_own, kv_other = pl.pallas_call(
        split_kernel,
        in_specs=[SMEM] + [pl.BlockSpec(memory_space=pltpu.HBM)] * 2,
        out_specs=[VMEM] * 2,
        out_shape=[pair, pair],
        scratch_shapes=[pltpu.SemaphoreType.DMA((4,))],
        compiler_params=BIG,
    )(place, keys, values)
    far = send(kv_own, to_far(0))
    cross = send(kv_other, to_far(1))
    mate = send(kv_other, to_mate)
    later_place, _ = lax.optimization_barrier((place, kv_own))

    lane = jnp.arange(128, dtype=jnp.int32)
    frequency = ROPE_BASE ** (-2.0 * (lane % 32).astype(jnp.float32) / ROTARY)
    tile = jax.ShapeDtypeStruct((TILE, DIM), jnp.bfloat16)
    table = jax.ShapeDtypeStruct((4 * ROWS, 128), jnp.float32)
    plan, cosine, sine, q_own, q_other = pl.pallas_call(
        prepare_kernel,
        in_specs=[SMEM] * 2 + [VMEM] * 3 + [pl.BlockSpec(memory_space=pltpu.HBM)],
        out_specs=[SMEM] + [VMEM] * 4,
        out_shape=[
            jax.ShapeDtypeStruct((4 * PER_TILE + 8,), jnp.int32),
            table,
            table,
            tile,
            tile,
        ],
        scratch_shapes=[
            pltpu.SMEM((36,), jnp.int32),
            pltpu.VMEM(queries.shape, jnp.bfloat16),
            pltpu.SemaphoreType.DMA((1,)),
        ],
        compiler_params=BIG,
    )(later_place, span_of, frequency.reshape(1, 128), q_gain, k_gain, queries)
    mate, far, cross, q_own, q_other = lax.optimization_barrier((mate, far, cross, q_own, q_other))

    base = pl.pallas_call(
        keys_kernel,
        in_specs=[VMEM] * 7,
        out_specs=VMEM,
        out_shape=jax.ShapeDtypeStruct((2, 2 * CHUNK, DIM), jnp.bfloat16),
        compiler_params=BIG,
    )(kv_own, mate, far, cross, k_gain, cosine, sine)

    rings = [base] + [send(base, to_ring(s, 0)) for s in SHIFTS[1:]]
    low, high = jnp.concatenate(rings[:2], axis=0), jnp.concatenate(rings[2:], axis=0)

    q_mine = jnp.stack(
        [q_own, send(q_other, to_mate), send(q_own, along_z(2)), send(q_other, along_z(-1))]
    ).reshape(2, 2 * TILE, DIM)
    low, high, q_mine = lax.optimization_barrier((low, high, q_mine))
    q_theirs = send(q_mine, to_core)
    first = [send(low, to_ring(1, 1)), send(high, to_ring(3, 1))]
    mine = attend(plan, q_mine, [low, high], [], 0, 0)
    low, high, mine = lax.optimization_barrier((low, high, mine))
    second = [send(high, to_ring(1, 1)), send(low, to_ring(3, 1))]
    theirs = attend(plan, q_theirs, [low, high], [], 0, 2)

    first, mine, theirs = lax.optimization_barrier((first, mine, theirs))
    last = [send(first[0], to_ring(1, 1)), send(first[1], to_ring(3, 1))]
    mine = attend(plan, q_mine, first, mine, 1, 0)
    theirs = attend(plan, q_theirs, first, theirs, 1, 2)
    second, mine, theirs = lax.optimization_barrier((second, mine, theirs))
    mine = attend(plan, q_mine, second, mine, 2, 0)
    theirs = attend(plan, q_theirs, second, theirs, 2, 2)
    last, mine, theirs = lax.optimization_barrier((last, mine, theirs))
    out_theirs = attend(plan, q_theirs, last, theirs, 3, 2)[0]
    received = send(out_theirs, to_core)
    out_mine = attend(plan, q_mine, last, mine, 3, 0)[0]

    joint = jax.ShapeDtypeStruct((TILE + STATS, DIM), jnp.bfloat16)
    parts = pl.pallas_call(
        join_kernel,
        in_specs=[VMEM] * 2,
        out_specs=[VMEM] * 4,
        out_shape=[joint] * 4,
        compiler_params=BIG,
    )(out_mine, received)
    home = [
        parts[0],
        send(parts[1], to_mate),
        send(parts[2], along_z(-2)),
        send(parts[3], along_z(-1)),
    ]

    return pl.pallas_call(
        finish_kernel,
        in_specs=[SMEM] + [VMEM] * 5,
        out_specs=VMEM,
        out_shape=jax.ShapeDtypeStruct(queries.shape, jnp.bfloat16),
        compiler_params=BIG,
    )(place, *home, gate)


def solution(mesh):
    rows = P(("blk", "uly"), None)
    in_specs = (rows, rows, rows, rows, P(), P(), P())
    return jax.shard_map(local, mesh=mesh, in_specs=in_specs, out_specs=rows, check_vma=False)
```

```python
import functools

import jax
import jax.numpy as jnp
from jax import lax
from jax.experimental import pallas as pl
from jax.experimental.pallas import tpu as pltpu
from jax.sharding import PartitionSpec as P

ROTARY = 64
ROPE_BASE = 10000000.0
EPSILON = 1e-06
LOG2E = 1.4426950408889634

GRID = (4, 2, 2, 4, 4)
AXES = ("blk", "uly")
ROWS = 64
DIM = 256
GROUP = 8
TILE = GROUP * ROWS
STATS = 16
SPAN = 512
CHUNK = 128
SHIFTS = (0, 1, 3, 2)

HIDDEN = -1e30
EMPTY = -1e25


def place_of(index):
    place = []
    for extent in reversed(GRID):
        place.append(index % extent)
        index //= extent
    return tuple(reversed(place))


def index_of(place):
    index = 0
    for extent, at in zip(GRID, place):
        index = index * extent + at
    return index


def send(array, target):
    count = index_of(tuple(extent - 1 for extent in GRID)) + 1
    route = [(i, index_of(target(*place_of(i)))) for i in range(count)]
    return lax.ppermute(array, AXES, route)


def to_mate(x, zh, c, y, zl):
    return (x, zh, c, y, zl ^ 1)


def to_far(flip):
    return lambda x, zh, c, y, zl: (x, zh ^ 1, c, y, zl ^ flip)


def along_z(even):
    def target(x, zh, c, y, zl):
        z = (zh * 4 + zl + (-even if zl & 1 else even)) % 8
        return (x, z // 4, c, y, z % 4)

    return target


def to_core(x, zh, c, y, zl):
    return (x, zh, c ^ 1, y, zl)


def to_ring(shift, phase):
    def target(x, zh, c, y, zl):
        if c == phase:
            return ((x + shift) % 4, zh, c, y, zl)
        return (x, zh, c, (y + shift) % 4, zl)

    return target


def whole(*shape):
    return pl.BlockSpec(shape, lambda *_: (0,) * len(shape))


def turned(piece, gain, cosine, sine):
    piece = piece.astype(jnp.float32)
    scale = lax.rsqrt(jnp.mean(piece * piece, axis=-1, keepdims=True) + EPSILON)
    piece = piece * scale * gain
    front = piece[:, :128]
    lane = lax.broadcasted_iota(jnp.int32, front.shape, 1)
    half = ROTARY // 2
    partner = jnp.where(lane < half, pltpu.roll(front, 128 - half, 1), pltpu.roll(front, half, 1))
    front = front * cosine + partner * sine
    return jnp.concatenate([front, piece[:, 128:]], axis=-1).astype(jnp.bfloat16)


def split_kernel(place, keys, values, own, other, done):
    side = place[4] & 1
    copies = []
    for n, (head, out) in enumerate(((side, own), (1 - side, other))):
        columns = pl.ds(pl.multiple_of(head * DIM, DIM), DIM)
        for m, source in enumerate((keys, values)):
            rows = pl.ds(m * ROWS, ROWS)
            copies.append(
                pltpu.make_async_copy(
                    source.at[:, columns], out.at[rows], done.at[2 * n + m]
                )
            )
    for copy in copies:
        copy.start()
    for copy in copies:
        copy.wait()


def ring_source(at, shift):
    return (at + 4 - shift) & 3


STAGES = ((0, 8), (8, 8), (16, 8), (24, 8))
PER_TILE = 72
NEVER = -(1 << 20)

ORDER = ((0, 0), (0, 4), (1, 0), (3, 4), (1, 4), (3, 0), (2, 0), (2, 4))


def prepare_kernel(
    place,
    span_of,
    frequency,
    gain,
    k_gain,
    queries,
    plan,
    cosine,
    sine,
    own,
    other,
    starts,
    fetched,
    done,
):
    fetch = pltpu.make_async_copy(queries, fetched, done.at[0])
    fetch.start()
    x, zh, c, y, zl = (place[n] for n in range(5))
    side = zl & 1

    def first_position(xs, zhs, cs, ys, within):
        slot = ((xs * 2 + zhs) * 2 + cs) * 2 + (ys >> 1)
        return span_of[slot] * SPAN + (ys & 1) * (SPAN // 2) + within

    z = zh * 4 + zl
    z_next = (z + jnp.where(side == 0, 7, 1)) & 7
    for core in range(2):
        for n, at in enumerate((z, z_next)):
            starts[2 * core + n] = first_position(
                x, at >> 2, c ^ core, y, ((at & 3) >> 1) * CHUNK
            )
    for a, (outer, low) in enumerate(ORDER):
        for b in range(4):
            inner = SHIFTS[(low + b) // 2]
            xs = jnp.where(c == 0, ring_source(x, inner), ring_source(x, outer))
            ys = jnp.where(c == 0, ring_source(y, outer), ring_source(y, inner))
            starts[4 + a * 4 + b] = first_position(
                xs, zh ^ (b & 1), c, ys, (zl >> 1) * CHUNK
            )

    row = lax.broadcasted_iota(jnp.int32, (ROWS, 128), 0)
    lane = lax.broadcasted_iota(jnp.int32, (ROWS, 128), 1)

    def rotation(first):
        angles = (row + first).astype(jnp.float32) * frequency[...]
        sines = jnp.sin(angles)
        sines = jnp.where(lane < ROTARY // 2, -sines, sines)
        rotated = lane < ROTARY
        return jnp.where(rotated, jnp.cos(angles), 1.0), jnp.where(rotated, sines, 0.0)

    for t in range(2):
        for n in range(2):
            rows = slice((2 * t + n) * ROWS, (2 * t + n + 1) * ROWS)
            cosine[rows], sine[rows] = rotation(starts[4 + t] + (side ^ n) * ROWS)
    q_cosine, q_sine = rotation(starts[0] + side * ROWS)
    fetch.wait()
    for head, out in ((side, own), (1 - side, other)):
        for member in range(GROUP):
            columns = pl.ds(pl.multiple_of((head * GROUP + member) * DIM, DIM), DIM)
            piece = turned(fetched[:, columns], gain[...], q_cosine, q_sine)
            out[member * ROWS : (member + 1) * ROWS] = piece * jnp.bfloat16(DIM**-0.5)

    for t in range(4):
        for stage, (first, chunks) in enumerate(STAGES):
            at = t * PER_TILE + first
            count = jnp.int32(0)
            for j in range(chunks):
                reach = starts[t] - starts[4 + first + j]
                plan[at + count] = j
                plan[at + 32 + count] = reach
                count += (reach > -CHUNK).astype(jnp.int32)
            plan[t * PER_TILE + 64 + stage] = count
    plan[4 * PER_TILE] = side
    bound = jnp.max(jnp.abs(gain[...])) * jnp.max(jnp.abs(k_gain[...])) * (16.0 * 1.02 * LOG2E)
    plan[4 * PER_TILE + 1] = (bound <= 100.0).astype(jnp.int32)


def keys_kernel(own, mate, far, cross, gain, cosine, sine, out):
    for n, piece in enumerate((own, mate, far, cross)):
        at = slice(n * ROWS, (n + 1) * ROWS)
        t, low = n // 2, (n % 2) * ROWS
        out[t, low : low + ROWS] = turned(piece[:ROWS], gain[...], cosine[at], sine[at])
        out[t, CHUNK + low : CHUNK + low + ROWS] = piece[ROWS:]


def attend_kernel(first, last, stages, pieces, width, buffers, plan, queries, *refs):
    stores, refs = refs[:buffers], list(refs[buffers:])
    if not first:
        del refs[:3]
    if last:
        out = refs.pop(0)
    top, total, acc = refs
    side = plan[4 * PER_TILE]
    bounded = plan[4 * PER_TILE + 1] == 1
    per_store = stores[0].shape[0]
    tiles = sorted({tile for _, tile, _ in pieces})

    if first:
        top[...] = jnp.full(top.shape, jnp.where(bounded, 0.0, EMPTY), jnp.float32)
        total[...] = jnp.zeros(total.shape, jnp.float32)
        acc[...] = jnp.zeros(acc.shape, jnp.float32)

    def fetch(j, part):
        rows = slice(part * CHUNK, (part + 1) * CHUNK)
        if buffers == 1:
            return stores[0][j, rows]
        within = lax.rem(j, per_store)
        picked = stores[0][within, rows]
        for n in range(1, buffers):
            picked = jnp.where(j >= n * per_store, stores[n][within, rows], picked)
        return picked

    def gather(tile, stage, n):
        base = tile * PER_TILE
        at = base + 8 * stage + width * n
        real = [width * n + m < plan[base + 64 + stage] for m in range(width)]
        skipped = 8 * (stage - stages[0])
        picks = [jnp.where(real[m], plan[at + m], 0) + skipped for m in range(width)]
        limits = [jnp.where(real[m], plan[at + 32 + m], NEVER) for m in range(width)]
        keys = jnp.concatenate([fetch(j, 0) for j in picks], axis=0)
        values = jnp.concatenate([fetch(j, 1) for j in picks], axis=0)
        return keys, values, limits

    def scores_of(place, rows, parity, keys, limits):
        block = queries[place, rows]
        scores = lax.dot_general(
            block, keys, (((1,), (1,)), ((), ())), preferred_element_type=jnp.float32
        )
        scores = scores * LOG2E
        row = lax.broadcasted_iota(jnp.int32, (block.shape[0], CHUNK), 0)
        lane = lax.broadcasted_iota(jnp.int32, (block.shape[0], CHUNK), 1)
        gap = (lane ^ (side * ROWS)) - (row & (ROWS - 1)) - (side ^ parity) * ROWS
        return [
            jnp.where(gap <= limit, scores[:, m * CHUNK : (m + 1) * CHUNK], HIDDEN)
            for m, limit in enumerate(limits)
        ]

    def add(p, rows, parts, values):
        weights = [jnp.exp2(part) for part in parts]
        total[p, rows] += functools.reduce(jnp.add, weights)
        acc[p, rows] += jnp.dot(
            jnp.concatenate(weights, axis=-1).astype(jnp.bfloat16),
            values,
            preferred_element_type=jnp.float32,
        )

    everything = slice(None)
    subs = TILE // 128

    def one_stage(stage):
        counts = [plan[tile * PER_TILE + 64 + stage] for tile in tiles]
        steps = lax.div(functools.reduce(jnp.maximum, counts) + (width - 1), width)

        @pl.when(bounded)
        def _():
            def step(n, carry):
                for tile in tiles:
                    keys, values, limits = gather(tile, stage, n)
                    for p, (place, its_tile, parity) in enumerate(pieces):
                        if its_tile == tile:
                            parts = scores_of(place, everything, parity, keys, limits)
                            add(p, everything, parts, values)
                return carry

            lax.fori_loop(0, steps, step, 0)

        @pl.when(jnp.logical_not(bounded))
        def _():
            def step(n, carry):
                p = lax.rem(lax.div(n, subs), len(pieces))
                place, tile, parity = pieces[0]
                for m in range(1, len(pieces)):
                    place = jnp.where(p == m, pieces[m][0], place)
                    tile = jnp.where(p == m, pieces[m][1], tile)
                    parity = jnp.where(p == m, pieces[m][2], parity)
                rows = pl.ds(pl.multiple_of(lax.rem(n, subs) * 128, 128), 128)
                keys, values, limits = gather(tile, stage, lax.div(n, subs * len(pieces)))
                parts = scores_of(place, rows, parity, keys, limits)
                before = top[p, rows]
                peak = functools.reduce(jnp.maximum, parts)
                now = jnp.maximum(before, jnp.max(peak, axis=-1, keepdims=True))
                fading = jnp.exp2(before - now)
                top[p, rows] = now
                total[p, rows] = total[p, rows] * fading
                acc[p, rows] = acc[p, rows] * jnp.concatenate([fading, fading], axis=-1)
                add(p, rows, [part - now for part in parts], values)
                return carry

            lax.fori_loop(0, subs * len(pieces) * steps, step, 0)

    if len(stages) == 1:
        one_stage(stages[0])
    else:
        lax.fori_loop(stages[0], stages[-1] + 1, lambda stage, carry: one_stage(stage) or carry, 0)

    if last:
        for p in range(len(pieces)):
            logs = []
            for sub in range(TILE // 128):
                rows = slice(sub * 128, (sub + 1) * 128)
                sums = jnp.sum(total[p, rows], axis=-1, keepdims=True)
                some = sums > 0.0
                sums = jnp.where(some, sums, 1.0)
                out[p, rows] = (acc[p, rows] / sums).astype(jnp.bfloat16)
                level = jnp.where(some, top[p, rows] + jnp.log2(sums), EMPTY)
                logs.append(level.T[:1])
            out[p, TILE:] = packed(logs)


def packed(logs):
    level = jnp.concatenate(logs, axis=0)
    high = level.astype(jnp.bfloat16).astype(jnp.float32)
    middle = (level - high).astype(jnp.bfloat16).astype(jnp.float32)
    low = level - high - middle
    rows = jnp.concatenate([high, middle, low, jnp.zeros_like(low)], axis=0)
    return jnp.concatenate([rows, jnp.zeros_like(rows)], axis=-1).astype(jnp.bfloat16)


def unpacked(rows):
    rows = rows[:, :128].astype(jnp.float32)
    return rows[0:4] + rows[4:8] + rows[8:12]


def blend(*parts):
    levels = [unpacked(part) for part in parts]
    peak = functools.reduce(jnp.maximum, levels)
    shares = [jnp.exp2(level - peak) for level in levels]
    whole = functools.reduce(jnp.add, shares)
    return [share / whole for share in shares], peak + jnp.log2(whole)


def column(shares, n):
    share = jnp.broadcast_to(shares[n : n + 1], (128, 128)).T
    return jnp.concatenate([share, share], axis=-1)


def blended(parts, shares, n):
    rows = slice(n * 128, (n + 1) * 128)
    return functools.reduce(
        jnp.add,
        [part[rows].astype(jnp.float32) * column(share, n) for part, share in zip(parts, shares)],
    )


def join_kernel(mine, theirs, *outs):
    for r, out in enumerate(outs):
        parts = (mine.at[r], theirs.at[r])
        shares, level = blend(*[part[TILE:] for part in parts])
        for n in range(TILE // 128):
            out[n * 128 : (n + 1) * 128] = blended(parts, shares, n).astype(jnp.bfloat16)
        out[TILE:] = packed([level])


def finish_kernel(place, mine, theirs, mate, far, beyond, gate, out):
    side = place[4] & 1
    for head, parts in ((1 - side, (mate, beyond)), (side, (far, mine, theirs))):
        shares, _ = blend(*[part[TILE:] for part in parts])
        for n in range(TILE // 128):
            attended = blended(parts, shares, n).astype(jnp.bfloat16).astype(jnp.float32)
            for m in range(2):
                at = (head * GROUP + 2 * n + m) * DIM
                columns = pl.ds(pl.multiple_of(at, DIM), DIM)
                logits = gate[:, columns].astype(jnp.float32)
                gated = attended[m * ROWS : (m + 1) * ROWS] * jax.nn.sigmoid(logits)
                out[:, columns] = gated.astype(jnp.bfloat16)


SMEM = pl.BlockSpec(memory_space=pltpu.SMEM)
VMEM = pl.BlockSpec(memory_space=pltpu.VMEM)
BIG = pltpu.CompilerParams(vmem_limit_bytes=28 * 1024 * 1024)


def attend(plan, queries, stores, state, stages, pieces, last, width=4, weight=1.0):
    count = len(pieces)
    shapes = [jax.ShapeDtypeStruct((count, TILE, width), jnp.float32) for width in (128, 128, DIM)]
    if last:
        shapes = [jax.ShapeDtypeStruct((count, TILE + STATS, DIM), jnp.bfloat16)] + shapes
    given = 2 + len(stores)
    chunks = 8 * len(stages)
    outs = pl.pallas_call(
        functools.partial(attend_kernel, not state, last, stages, pieces, width, len(stores)),
        in_specs=[SMEM] + [VMEM] * (1 + len(stores) + len(state)),
        out_specs=[VMEM] * len(shapes),
        out_shape=shapes,
        input_output_aliases={given + n: n + last for n in range(len(state))},
        compiler_params=BIG,
        cost_estimate=pl.CostEstimate(
            flops=int(4 * count * TILE * chunks * CHUNK * DIM * weight),
            bytes_accessed=int((4 << 20) * weight),
            transcendentals=int(count * TILE * chunks * CHUNK * weight),
        ),
    )(plan, queries, *stores, *state)
    return outs[0] if last else outs


def join(mine, theirs):
    joint = jax.ShapeDtypeStruct((TILE + STATS, DIM), jnp.bfloat16)
    return pl.pallas_call(
        join_kernel,
        in_specs=[VMEM] * 2,
        out_specs=[VMEM] * mine.shape[0],
        out_shape=[joint] * mine.shape[0],
        compiler_params=BIG,
    )(mine, theirs)


AWAY_MINE = ((1, 0, 1), (2, 1, 0), (3, 1, 1))
AWAY_THEIRS = ((1, 2, 1), (2, 3, 0), (3, 3, 1))
OWN = ((0, 0, 0), (1, 2, 0))


def local(queries, gate, keys, values, q_gain, k_gain, span_of):
    index = lax.axis_index("blk") * 16 + lax.axis_index("uly")
    place = jnp.stack(place_of(index)).astype(jnp.int32)
    q_gain, k_gain = q_gain.reshape(1, DIM), k_gain.reshape(1, DIM)

    pair = jax.ShapeDtypeStruct((2 * ROWS, DIM), jnp.bfloat16)
    kv_own, kv_other = pl.pallas_call(
        split_kernel,
        in_specs=[SMEM] + [pl.BlockSpec(memory_space=pltpu.HBM)] * 2,
        out_specs=[VMEM] * 2,
        out_shape=[pair, pair],
        scratch_shapes=[pltpu.SemaphoreType.DMA((4,))],
        compiler_params=BIG,
    )(place, keys, values)
    far = send(kv_own, to_far(0))
    cross = send(kv_other, to_far(1))
    mate = send(kv_other, to_mate)
    later_place, _ = lax.optimization_barrier((place, kv_own))

    lane = jnp.arange(128, dtype=jnp.int32)
    frequency = ROPE_BASE ** (-2.0 * (lane % 32).astype(jnp.float32) / ROTARY)
    tile = jax.ShapeDtypeStruct((TILE, DIM), jnp.bfloat16)
    table = jax.ShapeDtypeStruct((4 * ROWS, 128), jnp.float32)
    plan, cosine, sine, q_own, q_other = pl.pallas_call(
        prepare_kernel,
        in_specs=[SMEM] * 2 + [VMEM] * 3 + [pl.BlockSpec(memory_space=pltpu.HBM)],
        out_specs=[SMEM] + [VMEM] * 4,
        out_shape=[
            jax.ShapeDtypeStruct((4 * PER_TILE + 8,), jnp.int32),
            table,
            table,
            tile,
            tile,
        ],
        scratch_shapes=[
            pltpu.SMEM((36,), jnp.int32),
            pltpu.VMEM(queries.shape, jnp.bfloat16),
            pltpu.SemaphoreType.DMA((1,)),
        ],
        compiler_params=BIG,
    )(later_place, span_of, frequency.reshape(1, 128), q_gain, k_gain, queries)
    mate, far, cross, q_own, q_other = lax.optimization_barrier((mate, far, cross, q_own, q_other))

    base = pl.pallas_call(
        keys_kernel,
        in_specs=[VMEM] * 7,
        out_specs=VMEM,
        out_shape=jax.ShapeDtypeStruct((2, 2 * CHUNK, DIM), jnp.bfloat16),
        compiler_params=BIG,
    )(kv_own, mate, far, cross, k_gain, cosine, sine)

    rings = [base] + [send(base, to_ring(s, 0)) for s in SHIFTS[1:]]
    low, high = jnp.concatenate(rings[:2], axis=0), jnp.concatenate(rings[2:], axis=0)

    q_mine = jnp.stack(
        [q_own, send(q_other, to_mate), send(q_own, along_z(2)), send(q_other, along_z(-1))]
    )
    low, high, q_mine = lax.optimization_barrier((low, high, q_mine))
    q_theirs = send(q_mine, to_core)
    first = [send(low, to_ring(1, 1)), send(high, to_ring(3, 1))]
    mine = attend(plan, q_mine, [low, high], [], (0,), AWAY_MINE, False)
    low, high, mine = lax.optimization_barrier((low, high, mine))
    second = [send(high, to_ring(1, 1)), send(low, to_ring(3, 1))]
    theirs = attend(plan, q_theirs, [low, high], [], (0,), AWAY_THEIRS, False)

    first, mine, theirs = lax.optimization_barrier((first, mine, theirs))
    last = [send(first[0], to_ring(1, 1)), send(first[1], to_ring(3, 1))]
    mine = attend(plan, q_mine, first, mine, (1,), AWAY_MINE, False)
    theirs = attend(plan, q_theirs, first, theirs, (1,), AWAY_THEIRS, False)
    second, mine, theirs = lax.optimization_barrier((second, mine, theirs))
    mine = attend(plan, q_mine, second, mine, (2,), AWAY_MINE, False)
    theirs = attend(plan, q_theirs, second, theirs, (2,), AWAY_THEIRS, False)
    last, mine, theirs = lax.optimization_barrier((last, mine, theirs))
    out_theirs = attend(plan, q_theirs, last, theirs, (3,), AWAY_THEIRS, True)
    received = send(out_theirs, to_core)
    out_mine = attend(plan, q_mine, last, mine, (3,), AWAY_MINE, True)
    parts = join(out_mine, received)
    home = [
        send(parts[0], to_mate),
        send(parts[1], along_z(-2)),
        send(parts[2], along_z(-1)),
    ]

    stores, q_mine, q_theirs, _ = lax.optimization_barrier(
        ([low, high] + first + second + last, q_mine, q_theirs, parts)
    )
    out = attend(
        plan,
        jnp.stack([q_mine[0], q_theirs[0]]),
        [jnp.concatenate(stores, axis=0)],
        [],
        (0, 1, 2, 3),
        OWN,
        True,
        8,
        0.01,
    )
    home = [out[0], send(out[1], to_core), *home]

    return pl.pallas_call(
        finish_kernel,
        in_specs=[SMEM] + [VMEM] * 6,
        out_specs=VMEM,
        out_shape=jax.ShapeDtypeStruct(queries.shape, jnp.bfloat16),
        compiler_params=BIG,
    )(place, *home, gate)


def solution(mesh):
    rows = P(("blk", "uly"), None)
    in_specs = (rows, rows, rows, rows, P(), P(), P())
    return jax.shard_map(local, mesh=mesh, in_specs=in_specs, out_specs=rows, check_vma=False)
```

```python
import functools

import jax
import jax.numpy as jnp
from jax import lax
from jax.experimental import pallas as pl
from jax.experimental.pallas import tpu as pltpu
from jax.sharding import PartitionSpec as P

ROTARY = 64
ROPE_BASE = 10000000.0
EPSILON = 1e-06
LOG2E = 1.4426950408889634

GRID = (4, 2, 2, 4, 4)
AXES = ("blk", "uly")
ROWS = 64
DIM = 256
GROUP = 8
TILE = GROUP * ROWS
STATS = 16
SPAN = 512
CHUNK = 128
SHIFTS = (0, 1, 3, 2)

HIDDEN = -1e30
EMPTY = -1e25


def place_of(index):
    place = []
    for extent in reversed(GRID):
        place.append(index % extent)
        index //= extent
    return tuple(reversed(place))


def index_of(place):
    index = 0
    for extent, at in zip(GRID, place):
        index = index * extent + at
    return index


def send(array, target):
    count = index_of(tuple(extent - 1 for extent in GRID)) + 1
    route = [(i, index_of(target(*place_of(i)))) for i in range(count)]
    return lax.ppermute(array, AXES, route)


def to_mate(x, zh, c, y, zl):
    return (x, zh, c, y, zl ^ 1)


def to_far(flip):
    return lambda x, zh, c, y, zl: (x, zh ^ 1, c, y, zl ^ flip)


def along_z(even):
    def target(x, zh, c, y, zl):
        z = (zh * 4 + zl + (-even if zl & 1 else even)) % 8
        return (x, z // 4, c, y, z % 4)

    return target


def to_core(x, zh, c, y, zl):
    return (x, zh, c ^ 1, y, zl)


def to_ring(shift, phase):
    def target(x, zh, c, y, zl):
        if c == phase:
            return ((x + shift) % 4, zh, c, y, zl)
        return (x, zh, c, (y + shift) % 4, zl)

    return target


def whole(*shape):
    return pl.BlockSpec(shape, lambda *_: (0,) * len(shape))


def turned(piece, gain, cosine, sine):
    piece = piece.astype(jnp.float32)
    scale = lax.rsqrt(jnp.mean(piece * piece, axis=-1, keepdims=True) + EPSILON)
    piece = piece * scale * gain
    front = piece[:, :128]
    lane = lax.broadcasted_iota(jnp.int32, front.shape, 1)
    half = ROTARY // 2
    partner = jnp.where(lane < half, pltpu.roll(front, 128 - half, 1), pltpu.roll(front, half, 1))
    front = front * cosine + partner * sine
    return jnp.concatenate([front, piece[:, 128:]], axis=-1).astype(jnp.bfloat16)


def split_kernel(place, keys, values, own, other, done):
    side = place[4] & 1
    copies = []
    for n, (head, out) in enumerate(((side, own), (1 - side, other))):
        columns = pl.ds(pl.multiple_of(head * DIM, DIM), DIM)
        for m, source in enumerate((keys, values)):
            rows = pl.ds(m * ROWS, ROWS)
            copies.append(
                pltpu.make_async_copy(
                    source.at[:, columns], out.at[rows], done.at[2 * n + m]
                )
            )
    for copy in copies:
        copy.start()
    for copy in copies:
        copy.wait()


def ring_source(at, shift):
    return (at + 4 - shift) & 3


STAGES = ((0, 8), (8, 8), (16, 8), (24, 8))
PER_TILE = 72
NEVER = -(1 << 20)

ORDER = ((0, 0), (0, 4), (1, 0), (3, 4), (1, 4), (3, 0), (2, 0), (2, 4))


def prepare_kernel(
    place,
    span_of,
    frequency,
    gain,
    k_gain,
    queries,
    plan,
    cosine,
    sine,
    own,
    other,
    starts,
    fetched,
    done,
):
    fetch = pltpu.make_async_copy(queries, fetched, done.at[0])
    fetch.start()
    x, zh, c, y, zl = (place[n] for n in range(5))
    side = zl & 1

    def first_position(xs, zhs, cs, ys, within):
        slot = ((xs * 2 + zhs) * 2 + cs) * 2 + (ys >> 1)
        return span_of[slot] * SPAN + (ys & 1) * (SPAN // 2) + within

    z = zh * 4 + zl
    z_next = (z + jnp.where(side == 0, 7, 1)) & 7
    for core in range(2):
        for n, at in enumerate((z, z_next)):
            starts[2 * core + n] = first_position(
                x, at >> 2, c ^ core, y, ((at & 3) >> 1) * CHUNK
            )
    for a, (outer, low) in enumerate(ORDER):
        for b in range(4):
            inner = SHIFTS[(low + b) // 2]
            xs = jnp.where(c == 0, ring_source(x, inner), ring_source(x, outer))
            ys = jnp.where(c == 0, ring_source(y, outer), ring_source(y, inner))
            starts[4 + a * 4 + b] = first_position(
                xs, zh ^ (b & 1), c, ys, (zl >> 1) * CHUNK
            )

    row = lax.broadcasted_iota(jnp.int32, (ROWS, 128), 0)
    lane = lax.broadcasted_iota(jnp.int32, (ROWS, 128), 1)

    def rotation(first):
        angles = (row + first).astype(jnp.float32) * frequency[...]
        sines = jnp.sin(angles)
        sines = jnp.where(lane < ROTARY // 2, -sines, sines)
        rotated = lane < ROTARY
        return jnp.where(rotated, jnp.cos(angles), 1.0), jnp.where(rotated, sines, 0.0)

    for t in range(2):
        for n in range(2):
            rows = slice((2 * t + n) * ROWS, (2 * t + n + 1) * ROWS)
            cosine[rows], sine[rows] = rotation(starts[4 + t] + (side ^ n) * ROWS)
    q_cosine, q_sine = rotation(starts[0] + side * ROWS)
    fetch.wait()
    for head, out in ((side, own), (1 - side, other)):
        for member in range(GROUP):
            columns = pl.ds(pl.multiple_of((head * GROUP + member) * DIM, DIM), DIM)
            piece = turned(fetched[:, columns], gain[...], q_cosine, q_sine)
            out[member * ROWS : (member + 1) * ROWS] = piece * jnp.bfloat16(DIM**-0.5)

    for t in range(4):
        for stage, (first, chunks) in enumerate(STAGES):
            at = t * PER_TILE + first
            count = jnp.int32(0)
            for j in range(chunks):
                reach = starts[t] - starts[4 + first + j]
                plan[at + count] = j
                plan[at + 32 + count] = reach
                count += (reach > -CHUNK).astype(jnp.int32)
            plan[t * PER_TILE + 64 + stage] = count
    plan[4 * PER_TILE] = side
    bound = jnp.max(jnp.abs(gain[...])) * jnp.max(jnp.abs(k_gain[...])) * (16.0 * 1.02 * LOG2E)
    plan[4 * PER_TILE + 1] = (bound <= 100.0).astype(jnp.int32)


def keys_kernel(own, mate, far, cross, gain, cosine, sine, out):
    for n, piece in enumerate((own, mate, far, cross)):
        at = slice(n * ROWS, (n + 1) * ROWS)
        t, low = n // 2, (n % 2) * ROWS
        out[t, low : low + ROWS] = turned(piece[:ROWS], gain[...], cosine[at], sine[at])
        out[t, CHUNK + low : CHUNK + low + ROWS] = piece[ROWS:]


def attend_kernel(first, last, stages, pieces, width, buffers, plan, queries, *refs):
    stores, refs = refs[:buffers], list(refs[buffers:])
    if not first:
        del refs[:3]
    if last:
        out = refs.pop(0)
    top, total, acc = refs
    side = plan[4 * PER_TILE]
    bounded = plan[4 * PER_TILE + 1] == 1
    per_store = stores[0].shape[0]
    tiles = sorted({tile for _, tile, _ in pieces})

    if first:
        top[...] = jnp.full(top.shape, jnp.where(bounded, 0.0, EMPTY), jnp.float32)
        total[...] = jnp.zeros(total.shape, jnp.float32)
        acc[...] = jnp.zeros(acc.shape, jnp.float32)

    def fetch(j, part):
        rows = slice(part * CHUNK, (part + 1) * CHUNK)
        if buffers == 1:
            return stores[0][j, rows]
        within = lax.rem(j, per_store)
        picked = stores[0][within, rows]
        for n in range(1, buffers):
            picked = jnp.where(j >= n * per_store, stores[n][within, rows], picked)
        return picked

    def gather(tile, stage, n):
        base = tile * PER_TILE
        at = base + 8 * stage + width * n
        real = [width * n + m < plan[base + 64 + stage] for m in range(width)]
        skipped = 8 * (stage - stages[0])
        picks = [jnp.where(real[m], plan[at + m], 0) + skipped for m in range(width)]
        limits = [jnp.where(real[m], plan[at + 32 + m], NEVER) for m in range(width)]
        keys = jnp.concatenate([fetch(j, 0) for j in picks], axis=0)
        values = jnp.concatenate([fetch(j, 1) for j in picks], axis=0)
        return keys, values, limits

    def scores_of(place, rows, parity, keys, limits):
        block = queries[place, rows]
        scores = lax.dot_general(
            block, keys, (((1,), (1,)), ((), ())), preferred_element_type=jnp.float32
        )
        scores = scores * LOG2E
        row = lax.broadcasted_iota(jnp.int32, (block.shape[0], CHUNK), 0)
        lane = lax.broadcasted_iota(jnp.int32, (block.shape[0], CHUNK), 1)
        gap = (lane ^ (side * ROWS)) - (row & (ROWS - 1)) - (side ^ parity) * ROWS
        return [
            jnp.where(gap <= limit, scores[:, m * CHUNK : (m + 1) * CHUNK], HIDDEN)
            for m, limit in enumerate(limits)
        ]

    def add(p, rows, parts, values):
        weights = [jnp.exp2(part) for part in parts]
        total[p, rows] += functools.reduce(jnp.add, weights)
        acc[p, rows] += jnp.dot(
            jnp.concatenate(weights, axis=-1).astype(jnp.bfloat16),
            values,
            preferred_element_type=jnp.float32,
        )

    everything = slice(None)
    subs = TILE // 128

    def one_stage(stage):
        counts = [plan[tile * PER_TILE + 64 + stage] for tile in tiles]
        steps = lax.div(functools.reduce(jnp.maximum, counts) + (width - 1), width)

        @pl.when(bounded)
        def _():
            def step(n, carry):
                for tile in tiles:
                    keys, values, limits = gather(tile, stage, n)
                    for p, (place, its_tile, parity) in enumerate(pieces):
                        if its_tile == tile:
                            parts = scores_of(place, everything, parity, keys, limits)
                            add(p, everything, parts, values)
                return carry

            lax.fori_loop(0, steps, step, 0)

        @pl.when(jnp.logical_not(bounded))
        def _():
            def step(n, carry):
                p = lax.rem(lax.div(n, subs), len(pieces))
                place, tile, parity = pieces[0]
                for m in range(1, len(pieces)):
                    place = jnp.where(p == m, pieces[m][0], place)
                    tile = jnp.where(p == m, pieces[m][1], tile)
                    parity = jnp.where(p == m, pieces[m][2], parity)
                rows = pl.ds(pl.multiple_of(lax.rem(n, subs) * 128, 128), 128)
                keys, values, limits = gather(tile, stage, lax.div(n, subs * len(pieces)))
                parts = scores_of(place, rows, parity, keys, limits)
                before = top[p, rows]
                peak = functools.reduce(jnp.maximum, parts)
                now = jnp.maximum(before, jnp.max(peak, axis=-1, keepdims=True))
                fading = jnp.exp2(before - now)
                top[p, rows] = now
                total[p, rows] = total[p, rows] * fading
                acc[p, rows] = acc[p, rows] * jnp.concatenate([fading, fading], axis=-1)
                add(p, rows, [part - now for part in parts], values)
                return carry

            lax.fori_loop(0, subs * len(pieces) * steps, step, 0)

    if len(stages) == 1:
        one_stage(stages[0])
    else:
        lax.fori_loop(stages[0], stages[-1] + 1, lambda stage, carry: one_stage(stage) or carry, 0)

    if last:
        for p in range(len(pieces)):
            logs = []
            for sub in range(TILE // 128):
                rows = slice(sub * 128, (sub + 1) * 128)
                sums = jnp.sum(total[p, rows], axis=-1, keepdims=True)
                some = sums > 0.0
                sums = jnp.where(some, sums, 1.0)
                out[p, rows] = (acc[p, rows] / sums).astype(jnp.bfloat16)
                level = jnp.where(some, top[p, rows] + jnp.log2(sums), EMPTY)
                logs.append(level.T[:1])
            out[p, TILE:] = packed(logs)


def packed(logs):
    level = jnp.concatenate(logs, axis=0)
    high = level.astype(jnp.bfloat16).astype(jnp.float32)
    middle = (level - high).astype(jnp.bfloat16).astype(jnp.float32)
    low = level - high - middle
    rows = jnp.concatenate([high, middle, low, jnp.zeros_like(low)], axis=0)
    return jnp.concatenate([rows, jnp.zeros_like(rows)], axis=-1).astype(jnp.bfloat16)


def unpacked(rows):
    rows = rows[:, :128].astype(jnp.float32)
    return rows[0:4] + rows[4:8] + rows[8:12]


def blend(*parts):
    levels = [unpacked(part) for part in parts]
    peak = functools.reduce(jnp.maximum, levels)
    shares = [jnp.exp2(level - peak) for level in levels]
    whole = functools.reduce(jnp.add, shares)
    return [share / whole for share in shares], peak + jnp.log2(whole)


def column(shares, n):
    share = jnp.broadcast_to(shares[n : n + 1], (128, 128)).T
    return jnp.concatenate([share, share], axis=-1)


def blended(parts, shares, n):
    rows = slice(n * 128, (n + 1) * 128)
    return functools.reduce(
        jnp.add,
        [part[rows].astype(jnp.float32) * column(share, n) for part, share in zip(parts, shares)],
    )


def join_kernel(mine, theirs, *outs):
    for r, out in enumerate(outs):
        parts = (mine.at[r], theirs.at[r])
        shares, level = blend(*[part[TILE:] for part in parts])
        for n in range(TILE // 128):
            out[n * 128 : (n + 1) * 128] = blended(parts, shares, n).astype(jnp.bfloat16)
        out[TILE:] = packed([level])


def finish_kernel(place, mine, theirs, mate, far, beyond, gate, out):
    side = place[4] & 1
    for head, parts in ((1 - side, (mate, beyond)), (side, (far, mine, theirs))):
        shares, _ = blend(*[part[TILE:] for part in parts])
        for n in range(TILE // 128):
            attended = blended(parts, shares, n).astype(jnp.bfloat16).astype(jnp.float32)
            for m in range(2):
                at = (head * GROUP + 2 * n + m) * DIM
                columns = pl.ds(pl.multiple_of(at, DIM), DIM)
                logits = gate[:, columns].astype(jnp.float32)
                gated = attended[m * ROWS : (m + 1) * ROWS] * jax.nn.sigmoid(logits)
                out[:, columns] = gated.astype(jnp.bfloat16)


SMEM = pl.BlockSpec(memory_space=pltpu.SMEM)
VMEM = pl.BlockSpec(memory_space=pltpu.VMEM)
BIG = pltpu.CompilerParams(vmem_limit_bytes=28 * 1024 * 1024)


def attend(plan, queries, stores, state, stages, pieces, last, width=8, weight=1.0):
    count = len(pieces)
    shapes = [jax.ShapeDtypeStruct((count, TILE, width), jnp.float32) for width in (128, 128, DIM)]
    if last:
        shapes = [jax.ShapeDtypeStruct((count, TILE + STATS, DIM), jnp.bfloat16)] + shapes
    given = 2 + len(stores)
    chunks = 8 * len(stages)
    outs = pl.pallas_call(
        functools.partial(attend_kernel, not state, last, stages, pieces, width, len(stores)),
        in_specs=[SMEM] + [VMEM] * (1 + len(stores) + len(state)),
        out_specs=[VMEM] * len(shapes),
        out_shape=shapes,
        input_output_aliases={given + n: n + last for n in range(len(state))},
        compiler_params=BIG,
        cost_estimate=pl.CostEstimate(
            flops=int(4 * count * TILE * chunks * CHUNK * DIM * weight),
            bytes_accessed=int((4 << 20) * weight),
            transcendentals=int(count * TILE * chunks * CHUNK * weight),
        ),
    )(plan, queries, *stores, *state)
    return outs[0] if last else outs


def join(mine, theirs):
    joint = jax.ShapeDtypeStruct((TILE + STATS, DIM), jnp.bfloat16)
    return pl.pallas_call(
        join_kernel,
        in_specs=[VMEM] * 2,
        out_specs=[VMEM] * mine.shape[0],
        out_shape=[joint] * mine.shape[0],
        compiler_params=BIG,
    )(mine, theirs)


AWAY_MINE = ((1, 0, 1), (2, 1, 0), (3, 1, 1))
AWAY_THEIRS = ((1, 2, 1), (2, 3, 0), (3, 3, 1))
OWN = ((0, 0, 0), (1, 2, 0))


def local(queries, gate, keys, values, q_gain, k_gain, span_of):
    index = lax.axis_index("blk") * 16 + lax.axis_index("uly")
    place = jnp.stack(place_of(index)).astype(jnp.int32)
    q_gain, k_gain = q_gain.reshape(1, DIM), k_gain.reshape(1, DIM)

    pair = jax.ShapeDtypeStruct((2 * ROWS, DIM), jnp.bfloat16)
    kv_own, kv_other = pl.pallas_call(
        split_kernel,
        in_specs=[SMEM] + [pl.BlockSpec(memory_space=pltpu.HBM)] * 2,
        out_specs=[VMEM] * 2,
        out_shape=[pair, pair],
        scratch_shapes=[pltpu.SemaphoreType.DMA((4,))],
        compiler_params=BIG,
    )(place, keys, values)
    far = send(kv_own, to_far(0))
    cross = send(kv_other, to_far(1))
    mate = send(kv_other, to_mate)
    later_place, _ = lax.optimization_barrier((place, kv_own))

    lane = jnp.arange(128, dtype=jnp.int32)
    frequency = ROPE_BASE ** (-2.0 * (lane % 32).astype(jnp.float32) / ROTARY)
    tile = jax.ShapeDtypeStruct((TILE, DIM), jnp.bfloat16)
    table = jax.ShapeDtypeStruct((4 * ROWS, 128), jnp.float32)
    plan, cosine, sine, q_own, q_other = pl.pallas_call(
        prepare_kernel,
        in_specs=[SMEM] * 2 + [VMEM] * 3 + [pl.BlockSpec(memory_space=pltpu.HBM)],
        out_specs=[SMEM] + [VMEM] * 4,
        out_shape=[
            jax.ShapeDtypeStruct((4 * PER_TILE + 8,), jnp.int32),
            table,
            table,
            tile,
            tile,
        ],
        scratch_shapes=[
            pltpu.SMEM((36,), jnp.int32),
            pltpu.VMEM(queries.shape, jnp.bfloat16),
            pltpu.SemaphoreType.DMA((1,)),
        ],
        compiler_params=BIG,
    )(later_place, span_of, frequency.reshape(1, 128), q_gain, k_gain, queries)
    mate, far, cross, q_own, q_other = lax.optimization_barrier((mate, far, cross, q_own, q_other))

    base = pl.pallas_call(
        keys_kernel,
        in_specs=[VMEM] * 7,
        out_specs=VMEM,
        out_shape=jax.ShapeDtypeStruct((2, 2 * CHUNK, DIM), jnp.bfloat16),
        compiler_params=BIG,
    )(kv_own, mate, far, cross, k_gain, cosine, sine)

    rings = [base] + [send(base, to_ring(s, 0)) for s in SHIFTS[1:]]
    low, high = jnp.concatenate(rings[:2], axis=0), jnp.concatenate(rings[2:], axis=0)

    q_mine = jnp.stack(
        [q_own, send(q_other, to_mate), send(q_own, along_z(2)), send(q_other, along_z(-1))]
    )
    low, high, q_mine = lax.optimization_barrier((low, high, q_mine))
    q_theirs = send(q_mine, to_core)
    first = [send(low, to_ring(1, 1)), send(high, to_ring(3, 1))]
    mine = attend(plan, q_mine, [low, high], [], (0,), AWAY_MINE, False, 4)
    low, high, mine = lax.optimization_barrier((low, high, mine))
    second = [send(high, to_ring(1, 1)), send(low, to_ring(3, 1))]
    theirs = attend(plan, q_theirs, [low, high], [], (0,), AWAY_THEIRS, False, 4)

    first, mine, theirs = lax.optimization_barrier((first, mine, theirs))
    last = [send(first[0], to_ring(1, 1)), send(first[1], to_ring(3, 1))]
    mine = attend(plan, q_mine, first, mine, (1,), AWAY_MINE, False)
    theirs = attend(plan, q_theirs, first, theirs, (1,), AWAY_THEIRS, False)
    second, mine, theirs = lax.optimization_barrier((second, mine, theirs))
    mine = attend(plan, q_mine, second, mine, (2,), AWAY_MINE, False)
    theirs = attend(plan, q_theirs, second, theirs, (2,), AWAY_THEIRS, False)
    last, mine, theirs = lax.optimization_barrier((last, mine, theirs))
    out_theirs = attend(plan, q_theirs, last, theirs, (3,), AWAY_THEIRS, True)
    received = send(out_theirs, to_core)
    out_mine = attend(plan, q_mine, last, mine, (3,), AWAY_MINE, True)
    parts = join(out_mine, received)
    home = [
        send(parts[0], to_mate),
        send(parts[1], along_z(-2)),
        send(parts[2], along_z(-1)),
    ]

    stores, q_mine, q_theirs, _ = lax.optimization_barrier(
        ([low, high] + first + second + last, q_mine, q_theirs, parts)
    )
    out = attend(
        plan,
        jnp.stack([q_mine[0], q_theirs[0]]),
        [jnp.concatenate(stores, axis=0)],
        [],
        (0, 1, 2, 3),
        OWN,
        True,
        8,
        0.01,
    )
    home = [out[0], send(out[1], to_core), *home]

    return pl.pallas_call(
        finish_kernel,
        in_specs=[SMEM] + [VMEM] * 6,
        out_specs=VMEM,
        out_shape=jax.ShapeDtypeStruct(queries.shape, jnp.bfloat16),
        compiler_params=BIG,
    )(place, *home, gate)


def solution(mesh):
    rows = P(("blk", "uly"), None)
    in_specs = (rows, rows, rows, rows, P(), P(), P())
    return jax.shard_map(local, mesh=mesh, in_specs=in_specs, out_specs=rows, check_vma=False)
```

```python
import functools

import jax
import jax.numpy as jnp
from jax import lax
from jax.experimental import pallas as pl
from jax.experimental.pallas import tpu as pltpu
from jax.sharding import PartitionSpec as P

ROTARY = 64
ROPE_BASE = 10000000.0
EPSILON = 1e-06
LOG2E = 1.4426950408889634

GRID = (4, 2, 2, 4, 4)
AXES = ("blk", "uly")
ROWS = 64
DIM = 256
GROUP = 8
TILE = GROUP * ROWS
STATS = 16
SPAN = 512
CHUNK = 128
SHIFTS = (0, 1, 3, 2)

HIDDEN = -1e30
EMPTY = -1e25


def place_of(index):
    place = []
    for extent in reversed(GRID):
        place.append(index % extent)
        index //= extent
    return tuple(reversed(place))


def index_of(place):
    index = 0
    for extent, at in zip(GRID, place):
        index = index * extent + at
    return index


def send(array, target):
    count = index_of(tuple(extent - 1 for extent in GRID)) + 1
    route = [(i, index_of(target(*place_of(i)))) for i in range(count)]
    return lax.ppermute(array, AXES, route)


def to_mate(x, zh, c, y, zl):
    return (x, zh, c, y, zl ^ 1)


def to_far(flip):
    return lambda x, zh, c, y, zl: (x, zh ^ 1, c, y, zl ^ flip)


def along_z(even):
    def target(x, zh, c, y, zl):
        z = (zh * 4 + zl + (-even if zl & 1 else even)) % 8
        return (x, z // 4, c, y, z % 4)

    return target


def to_core(x, zh, c, y, zl):
    return (x, zh, c ^ 1, y, zl)


def to_ring(shift, phase):
    def target(x, zh, c, y, zl):
        if c == phase:
            return ((x + shift) % 4, zh, c, y, zl)
        return (x, zh, c, (y + shift) % 4, zl)

    return target


def whole(*shape):
    return pl.BlockSpec(shape, lambda *_: (0,) * len(shape))


def turned(piece, gain, cosine, sine):
    piece = piece.astype(jnp.float32)
    scale = lax.rsqrt(jnp.mean(piece * piece, axis=-1, keepdims=True) + EPSILON)
    piece = piece * scale * gain
    front = piece[:, :128]
    lane = lax.broadcasted_iota(jnp.int32, front.shape, 1)
    half = ROTARY // 2
    partner = jnp.where(lane < half, pltpu.roll(front, 128 - half, 1), pltpu.roll(front, half, 1))
    front = front * cosine + partner * sine
    return jnp.concatenate([front, piece[:, 128:]], axis=-1).astype(jnp.bfloat16)


def split_kernel(place, keys, values, own, other, done):
    side = place[4] & 1
    copies = []
    for n, (head, out) in enumerate(((side, own), (1 - side, other))):
        columns = pl.ds(pl.multiple_of(head * DIM, DIM), DIM)
        for m, source in enumerate((keys, values)):
            rows = pl.ds(m * ROWS, ROWS)
            copies.append(
                pltpu.make_async_copy(
                    source.at[:, columns], out.at[rows], done.at[2 * n + m]
                )
            )
    for copy in copies:
        copy.start()
    for copy in copies:
        copy.wait()


def ring_source(at, shift):
    return (at + 4 - shift) & 3


STAGES = ((0, 8), (8, 8), (16, 8), (24, 8))
PER_TILE = 72
NEVER = -(1 << 20)

ORDER = ((0, 0), (0, 4), (1, 0), (3, 4), (1, 4), (3, 0), (2, 0), (2, 4))


def prepare_kernel(
    place,
    span_of,
    frequency,
    gain,
    k_gain,
    queries,
    plan,
    cosine,
    sine,
    own,
    other,
    starts,
    fetched,
    done,
):
    fetch = pltpu.make_async_copy(queries, fetched, done.at[0])
    fetch.start()
    x, zh, c, y, zl = (place[n] for n in range(5))
    side = zl & 1

    def first_position(xs, zhs, cs, ys, within):
        slot = ((xs * 2 + zhs) * 2 + cs) * 2 + (ys >> 1)
        return span_of[slot] * SPAN + (ys & 1) * (SPAN // 2) + within

    z = zh * 4 + zl
    z_next = (z + jnp.where(side == 0, 7, 1)) & 7
    for core in range(2):
        for n, at in enumerate((z, z_next)):
            starts[2 * core + n] = first_position(
                x, at >> 2, c ^ core, y, ((at & 3) >> 1) * CHUNK
            )
    for a, (outer, low) in enumerate(ORDER):
        for b in range(4):
            inner = SHIFTS[(low + b) // 2]
            xs = jnp.where(c == 0, ring_source(x, inner), ring_source(x, outer))
            ys = jnp.where(c == 0, ring_source(y, outer), ring_source(y, inner))
            starts[4 + a * 4 + b] = first_position(
                xs, zh ^ (b & 1), c, ys, (zl >> 1) * CHUNK
            )

    row = lax.broadcasted_iota(jnp.int32, (ROWS, 128), 0)
    lane = lax.broadcasted_iota(jnp.int32, (ROWS, 128), 1)

    def rotation(first):
        angles = (row + first).astype(jnp.float32) * frequency[...]
        sines = jnp.sin(angles)
        sines = jnp.where(lane < ROTARY // 2, -sines, sines)
        rotated = lane < ROTARY
        return jnp.where(rotated, jnp.cos(angles), 1.0), jnp.where(rotated, sines, 0.0)

    for t in range(2):
        for n in range(2):
            rows = slice((2 * t + n) * ROWS, (2 * t + n + 1) * ROWS)
            cosine[rows], sine[rows] = rotation(starts[4 + t] + (side ^ n) * ROWS)
    q_cosine, q_sine = rotation(starts[0] + side * ROWS)
    fetch.wait()
    for head, out in ((side, own), (1 - side, other)):
        for member in range(GROUP):
            columns = pl.ds(pl.multiple_of((head * GROUP + member) * DIM, DIM), DIM)
            piece = turned(fetched[:, columns], gain[...], q_cosine, q_sine)
            out[member * ROWS : (member + 1) * ROWS] = piece * jnp.bfloat16(DIM**-0.5)

    for t in range(4):
        for stage, (first, chunks) in enumerate(STAGES):
            at = t * PER_TILE + first
            count = jnp.int32(0)
            for j in range(chunks):
                reach = starts[t] - starts[4 + first + j]
                plan[at + count] = j
                plan[at + 32 + count] = reach
                count += (reach > -CHUNK).astype(jnp.int32)
            plan[t * PER_TILE + 64 + stage] = count
    plan[4 * PER_TILE] = side
    bound = jnp.max(jnp.abs(gain[...])) * jnp.max(jnp.abs(k_gain[...])) * (16.0 * 1.02 * LOG2E)
    plan[4 * PER_TILE + 1] = (bound <= 100.0).astype(jnp.int32)


def keys_kernel(own, mate, far, cross, gain, cosine, sine, out):
    for n, piece in enumerate((own, mate, far, cross)):
        at = slice(n * ROWS, (n + 1) * ROWS)
        t, low = n // 2, (n % 2) * ROWS
        out[t, low : low + ROWS] = turned(piece[:ROWS], gain[...], cosine[at], sine[at])
        out[t, CHUNK + low : CHUNK + low + ROWS] = piece[ROWS:]


def attend_kernel(first, last, stages, pieces, width, buffers, plan, queries, *refs):
    stores, refs = refs[:buffers], list(refs[buffers:])
    if not first:
        del refs[:3]
    if last:
        out = refs.pop(0)
    top, total, acc = refs
    side = plan[4 * PER_TILE]
    bounded = plan[4 * PER_TILE + 1] == 1
    per_store = stores[0].shape[0]
    tiles = sorted({tile for _, tile, _ in pieces})

    if first:
        top[...] = jnp.full(top.shape, jnp.where(bounded, 0.0, EMPTY), jnp.float32)
        total[...] = jnp.zeros(total.shape, jnp.float32)
        acc[...] = jnp.zeros(acc.shape, jnp.float32)

    def fetch(j, part):
        rows = slice(part * CHUNK, (part + 1) * CHUNK)
        if buffers == 1:
            return stores[0][j, rows]
        within = lax.rem(j, per_store)
        picked = stores[0][within, rows]
        for n in range(1, buffers):
            picked = jnp.where(j >= n * per_store, stores[n][within, rows], picked)
        return picked

    def gather(tile, stage, n):
        base = tile * PER_TILE
        at = base + 8 * stage + width * n
        real = [width * n + m < plan[base + 64 + stage] for m in range(width)]
        skipped = 8 * (stage - stages[0])
        picks = [jnp.where(real[m], plan[at + m], 0) + skipped for m in range(width)]
        limits = [jnp.where(real[m], plan[at + 32 + m], NEVER) for m in range(width)]
        keys = jnp.concatenate([fetch(j, 0) for j in picks], axis=0)
        values = jnp.concatenate([fetch(j, 1) for j in picks], axis=0)
        return keys, values, limits

    def scores_of(place, rows, parity, keys, limits):
        block = queries[place, rows]
        scores = lax.dot_general(
            block, keys, (((1,), (1,)), ((), ())), preferred_element_type=jnp.float32
        )
        scores = scores * LOG2E
        row = lax.broadcasted_iota(jnp.int32, (block.shape[0], CHUNK), 0)
        lane = lax.broadcasted_iota(jnp.int32, (block.shape[0], CHUNK), 1)
        gap = (lane ^ (side * ROWS)) - (row & (ROWS - 1)) - (side ^ parity) * ROWS
        return [
            jnp.where(gap <= limit, scores[:, m * CHUNK : (m + 1) * CHUNK], HIDDEN)
            for m, limit in enumerate(limits)
        ]

    def add(p, rows, parts, values):
        weights = [jnp.exp2(part) for part in parts]
        total[p, rows] += functools.reduce(jnp.add, weights)
        acc[p, rows] += jnp.dot(
            jnp.concatenate(weights, axis=-1).astype(jnp.bfloat16),
            values,
            preferred_element_type=jnp.float32,
        )

    everything = slice(None)
    subs = TILE // 128

    def one_stage(stage):
        counts = [plan[tile * PER_TILE + 64 + stage] for tile in tiles]
        steps = lax.div(functools.reduce(jnp.maximum, counts) + (width - 1), width)

        @pl.when(bounded)
        def _():
            def step(n, carry):
                for tile in tiles:
                    keys, values, limits = gather(tile, stage, n)
                    for p, (place, its_tile, parity) in enumerate(pieces):
                        if its_tile == tile:
                            parts = scores_of(place, everything, parity, keys, limits)
                            add(p, everything, parts, values)
                return carry

            lax.fori_loop(0, steps, step, 0)

        @pl.when(jnp.logical_not(bounded))
        def _():
            def step(n, carry):
                p = lax.rem(lax.div(n, subs), len(pieces))
                place, tile, parity = pieces[0]
                for m in range(1, len(pieces)):
                    place = jnp.where(p == m, pieces[m][0], place)
                    tile = jnp.where(p == m, pieces[m][1], tile)
                    parity = jnp.where(p == m, pieces[m][2], parity)
                rows = pl.ds(pl.multiple_of(lax.rem(n, subs) * 128, 128), 128)
                keys, values, limits = gather(tile, stage, lax.div(n, subs * len(pieces)))
                parts = scores_of(place, rows, parity, keys, limits)
                before = top[p, rows]
                peak = functools.reduce(jnp.maximum, parts)
                now = jnp.maximum(before, jnp.max(peak, axis=-1, keepdims=True))
                fading = jnp.exp2(before - now)
                top[p, rows] = now
                total[p, rows] = total[p, rows] * fading
                acc[p, rows] = acc[p, rows] * jnp.concatenate([fading, fading], axis=-1)
                add(p, rows, [part - now for part in parts], values)
                return carry

            lax.fori_loop(0, subs * len(pieces) * steps, step, 0)

    if len(stages) == 1:
        one_stage(stages[0])
    else:
        lax.fori_loop(stages[0], stages[-1] + 1, lambda stage, carry: one_stage(stage) or carry, 0)

    if last:
        for p in range(len(pieces)):
            logs = []
            for sub in range(TILE // 128):
                rows = slice(sub * 128, (sub + 1) * 128)
                sums = jnp.sum(total[p, rows], axis=-1, keepdims=True)
                some = sums > 0.0
                sums = jnp.where(some, sums, 1.0)
                out[p, rows] = (acc[p, rows] / sums).astype(jnp.bfloat16)
                level = jnp.where(some, top[p, rows] + jnp.log2(sums), EMPTY)
                logs.append(level.T[:1])
            out[p, TILE:] = packed(logs)


def packed(logs):
    level = jnp.concatenate(logs, axis=0)
    high = level.astype(jnp.bfloat16).astype(jnp.float32)
    middle = (level - high).astype(jnp.bfloat16).astype(jnp.float32)
    low = level - high - middle
    rows = jnp.concatenate([high, middle, low, jnp.zeros_like(low)], axis=0)
    return jnp.concatenate([rows, jnp.zeros_like(rows)], axis=-1).astype(jnp.bfloat16)


def unpacked(rows):
    rows = rows[:, :128].astype(jnp.float32)
    return rows[0:4] + rows[4:8] + rows[8:12]


def blend(*parts):
    levels = [unpacked(part) for part in parts]
    peak = functools.reduce(jnp.maximum, levels)
    shares = [jnp.exp2(level - peak) for level in levels]
    whole = functools.reduce(jnp.add, shares)
    return [share / whole for share in shares], peak + jnp.log2(whole)


def column(shares, n):
    share = jnp.broadcast_to(shares[n : n + 1], (128, 128)).T
    return jnp.concatenate([share, share], axis=-1)


def blended(parts, shares, n):
    rows = slice(n * 128, (n + 1) * 128)
    return functools.reduce(
        jnp.add,
        [part[rows].astype(jnp.float32) * column(share, n) for part, share in zip(parts, shares)],
    )


def join_kernel(mine, theirs, *outs):
    for r, out in enumerate(outs):
        parts = (mine.at[r], theirs.at[r])
        shares, level = blend(*[part[TILE:] for part in parts])
        for n in range(TILE // 128):
            out[n * 128 : (n + 1) * 128] = blended(parts, shares, n).astype(jnp.bfloat16)
        out[TILE:] = packed([level])


def finish_kernel(place, mine, theirs, mate, far, beyond, gate, out):
    side = place[4] & 1
    for head, parts in ((1 - side, (mate, beyond)), (side, (far, mine, theirs))):
        shares, _ = blend(*[part[TILE:] for part in parts])
        for n in range(TILE // 128):
            attended = blended(parts, shares, n).astype(jnp.bfloat16).astype(jnp.float32)
            for m in range(2):
                at = (head * GROUP + 2 * n + m) * DIM
                columns = pl.ds(pl.multiple_of(at, DIM), DIM)
                logits = gate[:, columns].astype(jnp.float32)
                gated = attended[m * ROWS : (m + 1) * ROWS] * jax.nn.sigmoid(logits)
                out[:, columns] = gated.astype(jnp.bfloat16)


SMEM = pl.BlockSpec(memory_space=pltpu.SMEM)
VMEM = pl.BlockSpec(memory_space=pltpu.VMEM)
BIG = pltpu.CompilerParams(vmem_limit_bytes=28 * 1024 * 1024)


def attend(plan, queries, stores, state, stages, pieces, last, width=4, weight=1.0):
    count = len(pieces)
    shapes = [jax.ShapeDtypeStruct((count, TILE, width), jnp.float32) for width in (128, 128, DIM)]
    if last:
        shapes = [jax.ShapeDtypeStruct((count, TILE + STATS, DIM), jnp.bfloat16)] + shapes
    given = 2 + len(stores)
    chunks = 8 * len(stages)
    outs = pl.pallas_call(
        functools.partial(attend_kernel, not state, last, stages, pieces, width, len(stores)),
        in_specs=[SMEM] + [VMEM] * (1 + len(stores) + len(state)),
        out_specs=[VMEM] * len(shapes),
        out_shape=shapes,
        input_output_aliases={given + n: n + last for n in range(len(state))},
        compiler_params=BIG,
        cost_estimate=pl.CostEstimate(
            flops=int(4 * count * TILE * chunks * CHUNK * DIM * weight),
            bytes_accessed=int((4 << 20) * weight),
            transcendentals=int(count * TILE * chunks * CHUNK * weight),
        ),
    )(plan, queries, *stores, *state)
    return outs[0] if last else outs


def join(mine, theirs):
    joint = jax.ShapeDtypeStruct((TILE + STATS, DIM), jnp.bfloat16)
    return pl.pallas_call(
        join_kernel,
        in_specs=[VMEM] * 2,
        out_specs=[VMEM] * mine.shape[0],
        out_shape=[joint] * mine.shape[0],
        compiler_params=BIG,
    )(mine, theirs)


AWAY_MINE = ((1, 0, 1), (2, 1, 0), (3, 1, 1))
AWAY_THEIRS = ((1, 2, 1), (2, 3, 0), (3, 3, 1))
OWN = ((0, 0, 0), (1, 2, 0))


def local(queries, gate, keys, values, q_gain, k_gain, span_of):
    index = lax.axis_index("blk") * 16 + lax.axis_index("uly")
    place = jnp.stack(place_of(index)).astype(jnp.int32)
    q_gain, k_gain = q_gain.reshape(1, DIM), k_gain.reshape(1, DIM)

    pair = jax.ShapeDtypeStruct((2 * ROWS, DIM), jnp.bfloat16)
    kv_own, kv_other = pl.pallas_call(
        split_kernel,
        in_specs=[SMEM] + [pl.BlockSpec(memory_space=pltpu.HBM)] * 2,
        out_specs=[VMEM] * 2,
        out_shape=[pair, pair],
        scratch_shapes=[pltpu.SemaphoreType.DMA((4,))],
        compiler_params=BIG,
    )(place, keys, values)
    far = send(kv_own, to_far(0))
    cross = send(kv_other, to_far(1))
    mate = send(kv_other, to_mate)
    later_place, _ = lax.optimization_barrier((place, kv_own))

    lane = jnp.arange(128, dtype=jnp.int32)
    frequency = ROPE_BASE ** (-2.0 * (lane % 32).astype(jnp.float32) / ROTARY)
    tile = jax.ShapeDtypeStruct((TILE, DIM), jnp.bfloat16)
    table = jax.ShapeDtypeStruct((4 * ROWS, 128), jnp.float32)
    plan, cosine, sine, q_own, q_other = pl.pallas_call(
        prepare_kernel,
        in_specs=[SMEM] * 2 + [VMEM] * 3 + [pl.BlockSpec(memory_space=pltpu.HBM)],
        out_specs=[SMEM] + [VMEM] * 4,
        out_shape=[
            jax.ShapeDtypeStruct((4 * PER_TILE + 8,), jnp.int32),
            table,
            table,
            tile,
            tile,
        ],
        scratch_shapes=[
            pltpu.SMEM((36,), jnp.int32),
            pltpu.VMEM(queries.shape, jnp.bfloat16),
            pltpu.SemaphoreType.DMA((1,)),
        ],
        compiler_params=BIG,
    )(later_place, span_of, frequency.reshape(1, 128), q_gain, k_gain, queries)
    mate, far, cross, q_own, q_other = lax.optimization_barrier((mate, far, cross, q_own, q_other))

    base = pl.pallas_call(
        keys_kernel,
        in_specs=[VMEM] * 7,
        out_specs=VMEM,
        out_shape=jax.ShapeDtypeStruct((2, 2 * CHUNK, DIM), jnp.bfloat16),
        compiler_params=BIG,
    )(kv_own, mate, far, cross, k_gain, cosine, sine)

    rings = [base] + [send(base, to_ring(s, 0)) for s in SHIFTS[1:]]
    low, high = jnp.concatenate(rings[:2], axis=0), jnp.concatenate(rings[2:], axis=0)

    q_mine = jnp.stack(
        [q_own, send(q_other, to_mate), send(q_own, along_z(2)), send(q_other, along_z(-1))]
    )
    low, high, q_mine = lax.optimization_barrier((low, high, q_mine))
    q_theirs = send(q_mine, to_core)
    first = [send(low, to_ring(1, 1)), send(high, to_ring(3, 1))]
    mine = attend(plan, q_mine, [low, high], [], (0,), AWAY_MINE, False)
    low, high, mine = lax.optimization_barrier((low, high, mine))
    second = [send(high, to_ring(1, 1)), send(low, to_ring(3, 1))]
    theirs = attend(plan, q_theirs, [low, high], [], (0,), AWAY_THEIRS, False)

    first, mine, theirs = lax.optimization_barrier((first, mine, theirs))
    last = [send(first[0], to_ring(1, 1)), send(first[1], to_ring(3, 1))]
    mine = attend(plan, q_mine, first, mine, (1,), AWAY_MINE, False)
    theirs = attend(plan, q_theirs, first, theirs, (1,), AWAY_THEIRS, False)
    second, mine, theirs = lax.optimization_barrier((second, mine, theirs))
    mine = attend(plan, q_mine, second, mine, (2,), AWAY_MINE, False)
    theirs = attend(plan, q_theirs, second, theirs, (2,), AWAY_THEIRS, False)
    last, mine, theirs = lax.optimization_barrier((last, mine, theirs))
    out_theirs = attend(plan, q_theirs, last, theirs, (3,), AWAY_THEIRS, True, 8)
    received = send(out_theirs, to_core)
    out_mine = attend(plan, q_mine, last, mine, (3,), AWAY_MINE, True, 8)
    parts = join(out_mine, received)
    home = [
        send(parts[0], to_mate),
        send(parts[1], along_z(-2)),
        send(parts[2], along_z(-1)),
    ]

    stores, q_mine, q_theirs, _ = lax.optimization_barrier(
        ([low, high] + first + second + last, q_mine, q_theirs, parts)
    )
    out = attend(
        plan,
        jnp.stack([q_mine[0], q_theirs[0]]),
        [jnp.concatenate(stores, axis=0)],
        [],
        (0, 1, 2, 3),
        OWN,
        True,
        8,
        0.01,
    )
    home = [out[0], send(out[1], to_core), *home]

    return pl.pallas_call(
        finish_kernel,
        in_specs=[SMEM] + [VMEM] * 6,
        out_specs=VMEM,
        out_shape=jax.ShapeDtypeStruct(queries.shape, jnp.bfloat16),
        compiler_params=BIG,
    )(place, *home, gate)


def solution(mesh):
    rows = P(("blk", "uly"), None)
    in_specs = (rows, rows, rows, rows, P(), P(), P())
    return jax.shard_map(local, mesh=mesh, in_specs=in_specs, out_specs=rows, check_vma=False)
```
